128 devices in a mesh: blk: 64 (over z, y_lo, x, core), band: 2 (over y_hi).
Axes of the slice: x: 4, y: 4 (y_hi: 2, y_lo: 2; y = y_hi * 2 + y_lo), z: 4, core: 2. Of those that a mesh axis runs over, the one named last changes fastest.
Arguments:
- traces: bfloat16 [2048, 4096], P('blk'), may hold values from -6 to 6
- pair_list: int32 [16384, 2], P(('blk', 'band')), may hold values from 0 to 95, as said below
- counts: int32 [128], P(('blk', 'band')), may hold values from 16 to 128, as said below
- band_edges: int32 [4], replicated, may hold values from 1 to 2048, as said below
- observed: float32 [16384, 3, 512], P(('blk', 'band')), may hold values from -6 to 6
Outputs:
- adjoint: float32 [2048, 4096], P('blk', 'band')
- misfit: float32 [16384], P(('blk', 'band'))
The draws below stay inside these ranges and needn't reach their ends.
Inputs may be any that keep to these rules, and one draw needn't show every extreme that they name: pair_list[p, 0] < 32 and pair_list[p, 1] < 96; pair_list[p, 1] // 32 says whether the second channel lies in the owning block or one or two blocks before it on the cycle. `counts`: at most 128 used slots on a device, the used slots first; some device uses all 128. The edges rise strictly; band n covers bins band_edges[n] to band_edges[n + 1] - 1; the last edge is 2048.
All inputs are finite; a program needn't handle non-finite values.
Results may differ from the reference program's by a relative error of at most 0.011.
Values may be sent and summed in bfloat16 or wider, within the bound.
A program may use at most 192 MiB of HBM per device.

```python
import math
import jax
import jax.numpy as jnp
from jax import lax

SAMPLES = 4096
FREQ_BINS = 2048
MAX_LAG = 256
BAND_COUNT = 3
CHAN_DEV = 32
PAIR_CAP = 128
CHANNELS = 2048
PAIR_SLOTS = 16384
N_BLK = 64
N_BAND = 2


def draw_pair_list(key, part):
    key = jax.random.fold_in(key, 11)
    subkeys = jax.random.split(key, 2)
    first_col = jax.random.randint(subkeys[0], (PAIR_SLOTS, 1), 0, CHAN_DEV, dtype=jnp.int32)
    second_col = jax.random.randint(subkeys[1], (PAIR_SLOTS, 1), 0, 3 * CHAN_DEV, dtype=jnp.int32)
    return jnp.concatenate([first_col, second_col], axis=1)


def draw_counts(key, part):
    key = jax.random.fold_in(key, 12)
    device_total = PAIR_SLOTS // PAIR_CAP
    subkeys = jax.random.split(key, 3)
    light_load = jax.random.randint(subkeys[0], (device_total,), PAIR_CAP // 8, PAIR_CAP // 2 + 1, dtype=jnp.int32)
    heavy_load = jax.random.randint(subkeys[1], (device_total,), PAIR_CAP // 2, PAIR_CAP + 1, dtype=jnp.int32)
    ranking = jax.random.permutation(subkeys[2], device_total).astype(jnp.int32)
    pair_loads = jnp.where(ranking < max(1, device_total // 8), heavy_load, light_load)
    pair_loads = jnp.where(ranking == 0, PAIR_CAP, pair_loads)
    pair_loads = jnp.where(ranking == device_total - 1, PAIR_CAP // 8, pair_loads)
    return pair_loads.astype(jnp.int32)


def draw_band_edges(key, part):
    key = jax.random.fold_in(key, 13)
    subkeys = jax.random.split(key, 3)
    lowest = jax.random.randint(subkeys[0], (1,), 1, FREQ_BINS // 8 + 1, dtype=jnp.int32)
    lower_mid = jax.random.randint(subkeys[1], (1,), FREQ_BINS // 4, 3 * FREQ_BINS // 8 + 1, dtype=jnp.int32)
    upper_mid = jax.random.randint(subkeys[2], (1,), 5 * FREQ_BINS // 8, 3 * FREQ_BINS // 4 + 1, dtype=jnp.int32)
    highest = jnp.full((1,), FREQ_BINS, dtype=jnp.int32)
    return jnp.concatenate([lowest, lower_mid, upper_mid, highest], axis=0)


def block_scale(key, extent, shards, low, top_value):
    gain = 1.0
    for position, parts in shards:
        draws = jax.random.uniform(jax.random.fold_in(jax.random.fold_in(key, 6), position), (parts,), jnp.float32, low / len(shards), top_value / len(shards))
        gain = gain * jnp.repeat(jnp.exp(draws), extent[position] // parts).reshape((-1,) + (1,) * (len(extent) - 1 - position))
    return gain


def noise(rng, dims, scale, bound, cuts=(), kind=jnp.bfloat16):
    array = scale * jax.random.normal(rng, dims, jnp.float32)
    if cuts:
        array = array * block_scale(rng, dims, cuts, -0.22, 0.18)
    return jnp.clip(array, -bound, bound).astype(kind)


def setup_inputs(seed: int = 0) -> dict:
    streams_of = jax.random.split(jax.random.key(seed), 6)
    traces = noise(streams_of[0], (CHANNELS, SAMPLES), 1.0, 6.0, ((0, 64),))
    pair_list = draw_pair_list(jax.random.fold_in(streams_of[5], 71), 0)
    counts = draw_counts(jax.random.fold_in(streams_of[5], 71), 0)
    band_edges = draw_band_edges(jax.random.fold_in(streams_of[5], 71), 0)
    observed = noise(streams_of[4], (PAIR_SLOTS, BAND_COUNT, 2 * MAX_LAG), 1.0, 6.0, ((0, 128),), jnp.float32)
    return dict(traces=traces, pair_list=pair_list, counts=counts, band_edges=band_edges, observed=observed)


EPSILON = 1e-05

def basis_block(bin_ids, sample_ids):
    product = jnp.mod(sample_ids[:, None] * bin_ids[None, :], SAMPLES)
    phases = product.astype(jnp.float32) * (2.0 * math.pi / SAMPLES)
    return jnp.concatenate([jnp.cos(phases), -jnp.sin(phases)], axis=1).astype(jnp.bfloat16)

def lag_tables(band_edges):
    bin_ids = jnp.arange(FREQ_BINS, dtype=jnp.int32)
    shifts = jnp.arange(-MAX_LAG, MAX_LAG, dtype=jnp.int32)
    product = jnp.mod(bin_ids[:, None] * shifts[None, :], SAMPLES)
    phases = product.astype(jnp.float32) * (2.0 * math.pi / SAMPLES)
    lag_gain = 1.0 / math.sqrt(FREQ_BINS / 8.0)
    cosine = jnp.cos(phases) * lag_gain
    neg_sine = -jnp.sin(phases) * lag_gain
    tables = []
    for band_number in range(BAND_COUNT):
        inside = ((bin_ids >= band_edges[band_number]) & (bin_ids < band_edges[band_number + 1])).astype(jnp.float32)[:, None]
        tables.append(jnp.concatenate([inside * cosine, inside * neg_sine], axis=0).astype(jnp.bfloat16))
    return tables

def cross_spectrum(first_rows, second_rows):
    half_bins = first_rows.shape[1] // 2
    left_side = first_rows.astype(jnp.float32)
    right_side = second_rows.astype(jnp.float32)
    left_real, left_imag = (left_side[:, :half_bins], left_side[:, half_bins:])
    right_real, right_imag = (right_side[:, :half_bins], right_side[:, half_bins:])
    real_part = left_real * right_real + left_imag * right_imag
    imag_part = left_imag * right_real - left_real * right_imag
    return jnp.concatenate([real_part, imag_part], axis=1).astype(jnp.bfloat16)

def pair_grads(first_rows, second_rows, spec_grads):
    half_bins = first_rows.shape[1] // 2
    left_side = first_rows.astype(jnp.float32)
    right_side = second_rows.astype(jnp.float32)
    left_real, left_imag = (left_side[:, :half_bins], left_side[:, half_bins:])
    right_real, right_imag = (right_side[:, :half_bins], right_side[:, half_bins:])
    grad_real, grad_imag = (spec_grads[:, :half_bins], spec_grads[:, half_bins:])
    grad_first = jnp.concatenate([grad_real * right_real - grad_imag * right_imag, grad_real * right_imag + grad_imag * right_real], axis=1)
    grad_second = jnp.concatenate([grad_real * left_real + grad_imag * left_imag, grad_real * left_imag - grad_imag * left_real], axis=1)
    return (grad_first, grad_second)

def lag_adjoint(cross_rows, wanted, live_rows, tables):
    lag_gain = 1.0 / math.sqrt(FREQ_BINS / 8.0)
    spec_grads = None
    squares = None
    for band_number in range(len(tables)):
        table = tables[band_number]
        correlation = jnp.dot(cross_rows, table, preferred_element_type=jnp.float32)
        residual = (correlation - wanted[:, band_number, :]) * live_rows[:, None]
        band_squares = lax.optimization_barrier(jnp.sum(residual * residual, axis=1))
        squares = band_squares if squares is None else squares + band_squares
        weighted = (residual * lag_gain).astype(jnp.bfloat16)
        band_term = lax.dot_general(weighted, table, (((1,), (1,)), ((), ())), preferred_element_type=jnp.float32)
        spec_grads = band_term if spec_grads is None else spec_grads + band_term
    misfit = 0.5 * squares / (len(tables) * wanted.shape[2])
    return (misfit, spec_grads)

def reference(traces, pair_list, counts, band_edges, observed):
    values = traces.astype(jnp.float32)
    centred = values - lax.optimization_barrier(jnp.mean(values, axis=1, keepdims=True))
    spread = jnp.sqrt(lax.optimization_barrier(jnp.mean(centred * centred, axis=1, keepdims=True)) + EPSILON)
    normal_field = centred / spread
    whitened = normal_field.astype(jnp.bfloat16)
    spec_scale = 1.0 / math.sqrt(SAMPLES)
    all_ids = jnp.arange(FREQ_BINS, dtype=jnp.int32)
    basis = basis_block(all_ids, jnp.arange(SAMPLES, dtype=jnp.int32))
    spectra = (jnp.dot(whitened, basis, preferred_element_type=jnp.float32) * spec_scale).astype(jnp.bfloat16)
    tables = lag_tables(band_edges)
    device_total = N_BLK * N_BAND
    slot_ids = jnp.arange(PAIR_CAP, dtype=jnp.int32)

    def per_device(grads_sum, inputs):
        device, device_pairs, device_obs, device_count = inputs
        cycle_block = device // N_BAND
        first_ids = (cycle_block * CHAN_DEV + device_pairs[:, 0]).astype(jnp.int32)
        offset = device_pairs[:, 1] // CHAN_DEV
        second_ids = (jnp.mod(cycle_block - offset, N_BLK) * CHAN_DEV + jnp.mod(device_pairs[:, 1], CHAN_DEV)).astype(jnp.int32)
        live_rows = (slot_ids < device_count).astype(jnp.float32)
        first_rows = spectra[first_ids]
        second_rows = spectra[second_ids]
        cross_rows = cross_spectrum(first_rows, second_rows)
        misfit, spec_grads = lag_adjoint(cross_rows, device_obs, live_rows, tables)
        grad_first, grad_second = pair_grads(first_rows, second_rows, spec_grads)
        grads_sum = grads_sum.at[first_ids].add(grad_first).at[second_ids].add(grad_second)
        return (grads_sum, misfit)
    inputs = (jnp.arange(device_total, dtype=jnp.int32), pair_list.reshape(device_total, PAIR_CAP, 2), observed.reshape(device_total, PAIR_CAP, BAND_COUNT, 2 * MAX_LAG), counts)
    total_grads, misfit = lax.scan(per_device, jnp.zeros((CHANNELS, 2 * FREQ_BINS), jnp.float32), inputs)
    coeffs = total_grads.astype(jnp.bfloat16)
    time_field = lax.dot_general(coeffs, basis, (((1,), (1,)), ((), ())), preferred_element_type=jnp.float32) * spec_scale
    field_mean = lax.optimization_barrier(jnp.mean(time_field, axis=1, keepdims=True))
    cross_mean = lax.optimization_barrier(jnp.mean(time_field * normal_field, axis=1, keepdims=True))
    adjoint = (time_field - field_mean - normal_field * cross_mean) / spread
    return (adjoint, misfit.reshape(PAIR_SLOTS))
```

```python
import functools
import math

import jax
import jax.numpy as jnp
import ml_dtypes
import numpy as np
from jax import lax
from jax.experimental import pallas as pl
from jax.experimental.pallas import tpu as pltpu
from jax.sharding import PartitionSpec as P

SAMPLES = 4096
FREQ_BINS = 2048
MAX_LAG = 256
LAGS = 2 * MAX_LAG
BANDS = 3
CHAN = 32
PAIRS = 128
EPSILON = 1e-05
N1 = 16
N2 = 256
F2 = FREQ_BINS // N1
CHUNKS = 4
PER = N1 // CHUNKS
MESH = pl.DeviceIdType.MESH


def lag_table():
    f = np.arange(N1)[:, None] + N1 * np.arange(F2)[None, :]
    shift = np.arange(-MAX_LAG, MAX_LAG)
    angle = np.mod(f[:, :, None] * shift, SAMPLES) * (2.0 * np.pi / SAMPLES)
    rows = np.stack([np.cos(angle), -np.sin(angle)], axis=1) / math.sqrt(FREQ_BINS / 8.0)
    return rows.reshape(N1, 2 * F2, LAGS).astype(ml_dtypes.bfloat16)


def dft_table():
    angle = np.mod(np.arange(N2)[:, None] * np.arange(F2)[None, :], N2) * (2.0 * np.pi / N2)
    c, s = np.cos(angle), np.sin(angle)
    return np.block([[c, -s], [s, c]])


def twiddles():
    angle = np.arange(N1)[:, None] * np.arange(N2)[None, :] * (2.0 * np.pi / SAMPLES)
    return np.stack([np.cos(angle), np.sin(angle)], axis=1).astype(np.float32)


def combine(terms):
    total = None
    for gain, value in terms:
        if abs(gain) < 1e-9:
            continue
        if abs(abs(gain) - 1.0) < 1e-9:
            if total is None:
                total = value if gain > 0 else -value
            else:
                total = total + value if gain > 0 else total - value
        else:
            scaled = value * np.float32(gain)
            total = scaled if total is None else total + scaled
    return total


def cosine(k):
    return math.cos(2.0 * math.pi * k / 16)


def sine(k):
    return math.sin(2.0 * math.pi * k / 16)


def forward16(a):
    s = [a[j] + a[j + 8] for j in range(8)]
    d = [a[j] - a[j + 8] for j in range(8)]
    out = [None] * 9
    p = [None] + [d[j] - d[8 - j] for j in range(1, 4)]
    q = [None] + [d[j] + d[8 - j] for j in range(1, 4)]
    for f in (1, 3, 5, 7):
        real = combine([(1.0, d[0])] + [(cosine(j * f), p[j]) for j in range(1, 4)])
        imag = combine([(-sine(4 * f), d[4])] + [(-sine(j * f), q[j]) for j in range(1, 4)])
        out[f] = (real, imag)
    s2 = [s[j] + s[j + 4] for j in range(4)]
    d2 = [s[j] - s[j + 4] for j in range(4)]
    for f in (2, 6):
        real = combine([(1.0, d2[0]), (cosine(f), d2[1] - d2[3])])
        imag = combine([(-sine(2 * f), d2[2]), (-sine(f), d2[1] + d2[3])])
        out[f] = (real, imag)
    out[4] = (s2[0] - s2[2], s2[3] - s2[1])
    even, odd = s2[0] + s2[2], s2[1] + s2[3]
    out[0] = (even + odd, None)
    out[8] = (even - odd, None)
    return out


def inverse16(vr, vi):
    qr = [vr[0]] + [vr[f] + vr[16 - f] for f in range(1, 8)] + [vr[8]]
    qi = [None] + [vi[f] - vi[16 - f] for f in range(1, 8)]
    even, odd = [None] * 8, [None] * 8
    for t in range(5):
        ce = combine([(cosine(t * f), qr[f]) for f in (0, 2, 4, 6, 8)])
        se = combine([(sine(t * f), qi[f]) for f in (2, 4, 6)])
        co = combine([(cosine(t * f), qr[f]) for f in (1, 3, 5, 7)])
        so = combine([(sine(t * f), qi[f]) for f in (1, 3, 5, 7)])
        even[t] = ce if se is None else ce - se
        if co is None:
            odd[t] = -so
        else:
            odd[t] = co if so is None else co - so
        if 1 <= t <= 3:
            even[8 - t] = ce + se
            odd[8 - t] = -co - so
    return even, odd


def kernel(
    x_ref, pairs_ref, counts_ref, edges_ref, obs_hbm, tab_hbm, tabt_hbm, dft_hbm, idft_hbm, tw_hbm,
    adj_ref, mis_ref,
    tab, tabt, dft, idft, tw, obs, nf, z, reach, ab, xm, corr, wgt, own, psend, precv, v,
    field, fsend, frecv, ssend, srecv,
    load_sem, s_sem, r_sem, bs_sem, br_sem, x_ssem, x_rsem,
):
    blk = lax.axis_index("blk")
    band = lax.axis_index("band")
    n_blk = lax.axis_size("blk")

    def at(step):
        return (lax.rem(blk + step + n_blk, n_blk), band)

    partner = (blk, 1 - band)
    barrier = pltpu.get_barrier_semaphore()
    for where in (at(1), at(-1), at(2), at(-2), partner):
        pl.semaphore_signal(barrier, inc=1, device_id=where, device_id_type=MESH)

    loads = [
        pltpu.make_async_copy(src, dst, load_sem.at[i])
        for i, (src, dst) in enumerate(
            [(tw_hbm, tw), (dft_hbm, dft), (tab_hbm, tab), (obs_hbm, obs), (tabt_hbm, tabt), (idft_hbm, idft)]
        )
    ]
    for load in loads:
        load.start()

    values = x_ref[...].astype(jnp.float32)
    centred = values - jnp.mean(values, axis=1, keepdims=True)
    spread = jnp.sqrt(jnp.mean(centred * centred, axis=1, keepdims=True) + EPSILON)
    nf[...] = centred / spread

    chan_ids = lax.broadcasted_iota(jnp.int32, (128, PAIRS), 0)
    hits1 = (chan_ids == pairs_ref[0:1, :]).astype(jnp.float32)
    hits2 = (chan_ids == pairs_ref[1:2, :]).astype(jnp.float32)
    scatter = jnp.concatenate([hits1, hits2], axis=1).astype(jnp.bfloat16)[: 3 * CHAN]
    gather = jnp.concatenate([hits1.T, hits2.T], axis=0).astype(jnp.bfloat16)[:, : 3 * CHAN]

    loads[0].wait()
    for r in range(CHAN // 16):
        rows = slice(16 * r, 16 * r + 16)
        for h in range(N2 // 128):
            lanes = slice(128 * h, 128 * h + 128)
            a = [
                nf[rows, N2 * t + 128 * h : N2 * t + 128 * h + 128].astype(jnp.bfloat16).astype(jnp.float32)
                for t in range(N1)
            ]
            y = forward16(a)
            for f in range(N1):
                yr, yi = y[f] if f <= 8 else y[16 - f]
                c = tw[f, 0:1, lanes]
                s = tw[f, 1:2, lanes]
                if yi is None:
                    zr, zi = yr * c, -(yr * s)
                elif f <= 8:
                    zr, zi = yr * c + yi * s, yi * c - yr * s
                else:
                    zr, zi = yr * c - yi * s, -(yi * c) - yr * s
                z[32 * f + 16 * r : 32 * f + 16 * r + 16, lanes] = zr.astype(jnp.bfloat16)
                z[32 * f + 16 * r : 32 * f + 16 * r + 16, N2 + 128 * h : N2 + 128 * h + 128] = zi.astype(jnp.bfloat16)

    def spec_copy(g, hop):
        part = pl.ds(g * PER, PER)
        return pltpu.make_async_remote_copy(
            src_ref=reach.at[part, pl.ds(0, CHAN)],
            dst_ref=reach.at[part, pl.ds(CHAN * hop, CHAN)],
            send_sem=s_sem.at[hop - 1, g],
            recv_sem=r_sem.at[hop - 1, g],
            device_id=at(hop),
            device_id_type=MESH,
        )

    def grad_copy(g, hop):
        part = pl.ds(g * PER, PER)
        return pltpu.make_async_remote_copy(
            src_ref=psend.at[hop - 1, part],
            dst_ref=precv.at[hop - 1, part],
            send_sem=bs_sem.at[hop - 1, g],
            recv_sem=br_sem.at[hop - 1, g],
            device_id=at(-hop),
            device_id_type=MESH,
        )

    loads[1].wait()
    pl.semaphore_wait(barrier, 5)
    for g in range(CHUNKS):
        rows = PER * CHAN
        s = jnp.dot(z[rows * g : rows * (g + 1)], dft[...], preferred_element_type=jnp.float32)
        s = (s * (1.0 / math.sqrt(SAMPLES))).astype(jnp.bfloat16)
        reach[PER * g : PER * (g + 1), 0:CHAN, :] = s.reshape(PER, CHAN, 2 * F2)
        spec_copy(g, 1).start()
        spec_copy(g, 2).start()

    lane_bins = lax.broadcasted_iota(jnp.int32, (1, F2), 1) * N1

    def insides(f1):
        bins = lane_bins + f1
        return [(bins >= edges_ref[n]) & (bins < edges_ref[n + 1]) for n in range(BANDS)]

    loads[2].wait()
    corr[...] = jnp.zeros_like(corr)

    def correlate(g, carry):
        spec_copy(g, 1).wait_recv()
        spec_copy(g, 2).wait_recv()
        for i in range(PER):
            f1 = g * PER + i
            both = jnp.dot(gather, reach[f1], preferred_element_type=jnp.float32)
            ab[f1] = both.astype(jnp.bfloat16)
            ar, ai = both[:PAIRS, :F2], both[:PAIRS, F2:]
            br, bi = both[PAIRS:, :F2], both[PAIRS:, F2:]
            xr = ar * br + ai * bi
            xi = ai * br - ar * bi
            for n, inside in enumerate(insides(f1)):
                rows = slice(PAIRS * n, PAIRS * (n + 1))
                xm[rows, 2 * F2 * i : 2 * F2 * i + F2] = jnp.where(inside, xr, 0.0).astype(jnp.bfloat16)
                xm[rows, 2 * F2 * i + F2 : 2 * F2 * (i + 1)] = jnp.where(inside, xi, 0.0).astype(jnp.bfloat16)
        part = tab[pl.ds(g * PER, PER)].reshape(PER * 2 * F2, LAGS)
        corr[...] += jnp.dot(xm[...], part, preferred_element_type=jnp.float32)
        return carry

    lax.fori_loop(0, CHUNKS, correlate, 0)

    loads[3].wait()
    slot = lax.broadcasted_iota(jnp.int32, (PAIRS, 1), 0)
    live = (slot < counts_ref[0]).astype(jnp.float32)
    squares = jnp.zeros((PAIRS, 1), jnp.float32)
    for n in range(BANDS):
        rows = slice(PAIRS * n, PAIRS * (n + 1))
        residual = (corr[rows] - obs[n]) * live
        squares = squares + jnp.sum(residual * residual, axis=1, keepdims=True)
        wgt[rows] = (residual * (1.0 / math.sqrt(FREQ_BINS / 8.0))).astype(jnp.bfloat16)
    misfit = squares * (0.5 / (BANDS * LAGS))
    mis_ref[...] = jnp.broadcast_to(misfit, (PAIRS, PAIRS)).T[0:1]

    loads[4].wait()

    def spread_back(g, carry):
        for i in range(PER):
            f1 = g * PER + i
            raw = jnp.dot(wgt[...], tabt[f1], preferred_element_type=jnp.float32)
            ins = [jnp.concatenate([m, m], axis=1) for m in insides(f1)]
            grad = jnp.where(ins[0], raw[0:PAIRS], 0.0)
            grad = jnp.where(ins[1], raw[PAIRS : 2 * PAIRS], grad)
            grad = jnp.where(ins[2], raw[2 * PAIRS :], grad)
            gr, gi = grad[:, :F2], grad[:, F2:]
            both = ab[f1].astype(jnp.float32)
            ar, ai = both[:PAIRS, :F2], both[:PAIRS, F2:]
            br, bi = both[PAIRS:, :F2], both[PAIRS:, F2:]
            first = jnp.concatenate([gr * br - gi * bi, gr * bi + gi * br], axis=1)
            second = jnp.concatenate([gr * ar + gi * ai, gr * ai - gi * ar], axis=1)
            grads = jnp.concatenate([first, second], axis=0).astype(jnp.bfloat16)
            sums = jnp.dot(scatter, grads, preferred_element_type=jnp.float32)
            own[f1] = sums[:CHAN]
            psend[0, f1] = sums[CHAN : 2 * CHAN].astype(jnp.bfloat16)
            psend[1, f1] = sums[2 * CHAN :].astype(jnp.bfloat16)
        grad_copy(g, 1).start()
        grad_copy(g, 2).start()
        return carry

    lax.fori_loop(0, CHUNKS, spread_back, 0)

    loads[5].wait()

    def invert(g, carry):
        grad_copy(g, 1).wait_recv()
        grad_copy(g, 2).wait_recv()
        part = pl.ds(g * PER, PER)
        total = own[part] + precv[0, part].astype(jnp.float32) + precv[1, part].astype(jnp.float32)
        coeffs = total.astype(jnp.bfloat16).reshape(PER * CHAN, 2 * F2)
        u = jnp.dot(coeffs, idft[...], preferred_element_type=jnp.float32)
        for i in range(PER):
            f1 = g * PER + i
            ur, ui = u[CHAN * i : CHAN * (i + 1), :N2], u[CHAN * i : CHAN * (i + 1), N2:]
            c, s = tw[f1, 0:1], tw[f1, 1:2]
            v[f1, 0] = ur * c - ui * s
            v[f1, 1] = ur * s + ui * c
        return carry

    lax.fori_loop(0, CHUNKS, invert, 0)

    sign = (1 - 2 * band).astype(jnp.float32)
    half = N1 // 2 * N2
    for r in range(CHAN // 16):
        rows = slice(16 * r, 16 * r + 16)
        total_e = jnp.zeros((16, 128), jnp.float32)
        total_w = jnp.zeros((16, 128), jnp.float32)
        for h in range(N2 // 128):
            lanes = slice(128 * h, 128 * h + 128)
            vr = [v[f, 0, rows, lanes] for f in range(N1)]
            vi = [v[f, 1, rows, lanes] for f in range(N1)]
            even, odd = inverse16(vr, vi)
            for t in range(8):
                lo = N2 * t + 128 * h
                out = slice(lo, lo + 128)
                total_e = total_e + even[t]
                low, high = nf[rows, out], nf[rows, half + lo : half + lo + 128]
                total_w = total_w + (even[t] * (low + high) + odd[t] * (low - high))
                mine = odd[t] * sign
                field[rows, out] = even[t] + mine
                fsend[rows, out] = (even[t] - mine).astype(jnp.bfloat16)
        sum_u = jnp.sum(total_e, axis=1, keepdims=True) * (2.0 / SAMPLES)
        sum_w = jnp.sum(total_w, axis=1, keepdims=True) * (1.0 / SAMPLES)
        ssend[rows, 0:128] = jnp.broadcast_to(sum_u, (16, 128))
        ssend[rows, 128:256] = jnp.broadcast_to(sum_w, (16, 128))

    swaps = [
        pltpu.make_async_remote_copy(
            src_ref=src, dst_ref=dst, send_sem=x_ssem.at[i], recv_sem=x_rsem.at[i],
            device_id=partner, device_id_type=MESH,
        )
        for i, (src, dst) in enumerate([(ssend, srecv), (fsend, frecv)])
    ]
    for swap in swaps:
        swap.start()
    for swap in swaps:
        swap.wait()
    mean_u = ssend[:, 0:1] + srecv[:, 0:1]
    mean_w = ssend[:, 128:129] + srecv[:, 128:129]
    mine = nf[:, pl.ds(pl.multiple_of(band * half, half), half)]
    adj_ref[...] = (field[...] + frecv[...].astype(jnp.float32) - mean_u - mine * mean_w) / spread

    def drain(g, carry):
        for hop in (1, 2):
            spec_copy(g, hop).wait_send()
            grad_copy(g, hop).wait_send()
        return carry

    lax.fori_loop(0, CHUNKS, drain, 0)


def per_device(traces, pair_list, counts, band_edges, observed):
    bf16, f32 = jnp.bfloat16, jnp.float32
    table = lag_table()
    dft = dft_table()
    tables = [
        jnp.asarray(table),
        jnp.asarray(np.ascontiguousarray(np.swapaxes(table, 1, 2))),
        jnp.asarray(dft.astype(ml_dtypes.bfloat16)),
        jnp.asarray((dft.T / math.sqrt(SAMPLES)).astype(ml_dtypes.bfloat16)),
        jnp.asarray(twiddles()),
    ]
    vmem = pl.BlockSpec(memory_space=pltpu.VMEM)
    smem = pl.BlockSpec(memory_space=pltpu.SMEM)
    hbm = pl.BlockSpec(memory_space=pl.ANY)
    dma = pltpu.SemaphoreType.DMA
    adjoint, misfit = pl.pallas_call(
        kernel,
        out_shape=(
            jax.ShapeDtypeStruct((CHAN, SAMPLES // 2), f32),
            jax.ShapeDtypeStruct((1, PAIRS), f32),
        ),
        in_specs=[vmem, vmem, smem, smem] + [hbm] * 6,
        out_specs=(vmem, vmem),
        scratch_shapes=[
            pltpu.VMEM((N1, 2 * F2, LAGS), bf16),
            pltpu.VMEM((N1, LAGS, 2 * F2), bf16),
            pltpu.VMEM((2 * N2, 2 * F2), bf16),
            pltpu.VMEM((2 * F2, 2 * N2), bf16),
            pltpu.VMEM((N1, 2, N2), f32),
            pltpu.VMEM((BANDS, PAIRS, LAGS), f32),
            pltpu.VMEM((CHAN, SAMPLES), f32),
            pltpu.VMEM((N1 * CHAN, 2 * N2), bf16),
            pltpu.VMEM((N1, 3 * CHAN, 2 * F2), bf16),
            pltpu.VMEM((N1, 2 * PAIRS, 2 * F2), bf16),
            pltpu.VMEM((BANDS * PAIRS, PER * 2 * F2), bf16),
            pltpu.VMEM((BANDS * PAIRS, LAGS), f32),
            pltpu.VMEM((BANDS * PAIRS, LAGS), bf16),
            pltpu.VMEM((N1, CHAN, 2 * F2), f32),
            pltpu.VMEM((2, N1, CHAN, 2 * F2), bf16),
            pltpu.VMEM((2, N1, CHAN, 2 * F2), bf16),
            pltpu.VMEM((N1, 2, CHAN, N2), f32),
            pltpu.VMEM((CHAN, SAMPLES // 2), f32),
            pltpu.VMEM((CHAN, SAMPLES // 2), bf16),
            pltpu.VMEM((CHAN, SAMPLES // 2), bf16),
            pltpu.VMEM((CHAN, 256), f32),
            pltpu.VMEM((CHAN, 256), f32),
            dma((6,)),
            dma((2, CHUNKS)),
            dma((2, CHUNKS)),
            dma((2, CHUNKS)),
            dma((2, CHUNKS)),
            dma((2,)),
            dma((2,)),
        ],
        compiler_params=pltpu.CompilerParams(
            collective_id=0, has_side_effects=True, vmem_limit_bytes=48 << 20
        ),
        name="misfit_adjoint",
    )(traces, pair_list.T, counts, band_edges, jnp.transpose(observed, (1, 0, 2)), *tables)
    return adjoint, misfit.reshape(PAIRS)


def solution(mesh):
    in_specs = (
        P("blk", None),
        P(("blk", "band"), None),
        P(("blk", "band")),
        P(),
        P(("blk", "band"), None, None),
    )
    out_specs = (P("blk", "band"), P(("blk", "band")))
    return jax.shard_map(
        per_device, mesh=mesh, in_specs=in_specs, out_specs=out_specs, check_vma=False
    )
```

```python
import functools
import math

import jax
import jax.numpy as jnp
import ml_dtypes
import numpy as np
from jax import lax
from jax.experimental import pallas as pl
from jax.experimental.pallas import tpu as pltpu
from jax.sharding import PartitionSpec as P

SAMPLES = 4096
FREQ_BINS = 2048
MAX_LAG = 256
LAGS = 2 * MAX_LAG
BANDS = 3
CHAN = 32
PAIRS = 128
EPSILON = 1e-05
N1 = 16
N2 = 256
F2 = FREQ_BINS // N1
CHUNKS = 4
PER = N1 // CHUNKS
MESH = pl.DeviceIdType.MESH


def lag_table():
    f = np.arange(N1)[:, None] + N1 * np.arange(F2)[None, :]
    shift = np.arange(-MAX_LAG, MAX_LAG)
    angle = np.mod(f[:, :, None] * shift, SAMPLES) * (2.0 * np.pi / SAMPLES)
    rows = np.stack([np.cos(angle), -np.sin(angle)], axis=1) / math.sqrt(FREQ_BINS / 8.0)
    return rows.reshape(N1, 2 * F2, LAGS).astype(ml_dtypes.bfloat16)


def dft_table():
    angle = np.mod(np.arange(N2)[:, None] * np.arange(F2)[None, :], N2) * (2.0 * np.pi / N2)
    c, s = np.cos(angle), np.sin(angle)
    return np.block([[c, -s], [s, c]])


def twiddles():
    angle = np.arange(N1)[:, None] * np.arange(N2)[None, :] * (2.0 * np.pi / SAMPLES)
    return np.stack([np.cos(angle), np.sin(angle)], axis=1).astype(np.float32)


def combine(terms):
    total = None
    for gain, value in terms:
        if abs(gain) < 1e-9:
            continue
        if abs(abs(gain) - 1.0) < 1e-9:
            if total is None:
                total = value if gain > 0 else -value
            else:
                total = total + value if gain > 0 else total - value
        else:
            scaled = value * np.float32(gain)
            total = scaled if total is None else total + scaled
    return total


def cosine(k):
    return math.cos(2.0 * math.pi * k / 16)


def sine(k):
    return math.sin(2.0 * math.pi * k / 16)


def forward16(a):
    s = [a[j] + a[j + 8] for j in range(8)]
    d = [a[j] - a[j + 8] for j in range(8)]
    out = [None] * 9
    p = [None] + [d[j] - d[8 - j] for j in range(1, 4)]
    q = [None] + [d[j] + d[8 - j] for j in range(1, 4)]
    for f in (1, 3, 5, 7):
        real = combine([(1.0, d[0])] + [(cosine(j * f), p[j]) for j in range(1, 4)])
        imag = combine([(-sine(4 * f), d[4])] + [(-sine(j * f), q[j]) for j in range(1, 4)])
        out[f] = (real, imag)
    s2 = [s[j] + s[j + 4] for j in range(4)]
    d2 = [s[j] - s[j + 4] for j in range(4)]
    for f in (2, 6):
        real = combine([(1.0, d2[0]), (cosine(f), d2[1] - d2[3])])
        imag = combine([(-sine(2 * f), d2[2]), (-sine(f), d2[1] + d2[3])])
        out[f] = (real, imag)
    out[4] = (s2[0] - s2[2], s2[3] - s2[1])
    even, odd = s2[0] + s2[2], s2[1] + s2[3]
    out[0] = (even + odd, None)
    out[8] = (even - odd, None)
    return out


def inverse16(vr, vi):
    qr = [vr[0]] + [vr[f] + vr[16 - f] for f in range(1, 8)] + [vr[8]]
    qi = [None] + [vi[f] - vi[16 - f] for f in range(1, 8)]
    even, odd = [None] * 8, [None] * 8
    for t in range(5):
        ce = combine([(cosine(t * f), qr[f]) for f in (0, 2, 4, 6, 8)])
        se = combine([(sine(t * f), qi[f]) for f in (2, 4, 6)])
        co = combine([(cosine(t * f), qr[f]) for f in (1, 3, 5, 7)])
        so = combine([(sine(t * f), qi[f]) for f in (1, 3, 5, 7)])
        even[t] = ce if se is None else ce - se
        if co is None:
            odd[t] = -so
        else:
            odd[t] = co if so is None else co - so
        if 1 <= t <= 3:
            even[8 - t] = ce + se
            odd[8 - t] = -co - so
    return even, odd


def kernel(
    x_hbm, pairs_hbm, counts_hbm, edges_hbm, obs_hbm, tab_hbm, tabt_hbm, dft_hbm, idft_hbm, tw_hbm,
    adj_ref, mis_ref,
    x_ref, pairs_ref, counts_ref, edges_ref, tab, tabt, dft, idft, tw, obs, nf, z, reach, ab, xm, corr, wgt, raw, own, psend, precv, v,
    field, fsend, frecv, ssend, srecv,
    load_sem, s_sem, r_sem, bs_sem, br_sem, x_ssem, x_rsem,
):
    blk = lax.axis_index("blk")
    band = lax.axis_index("band")
    n_blk = lax.axis_size("blk")

    def at(step):
        return (lax.rem(blk + step + n_blk, n_blk), band)

    partner = (blk, 1 - band)
    barrier = pltpu.get_barrier_semaphore()
    for where in (at(1), at(-1), at(2), at(-2), partner):
        pl.semaphore_signal(barrier, inc=1, device_id=where, device_id_type=MESH)

    loads = {
        name: pltpu.make_async_copy(src, dst, load_sem.at[i])
        for i, (name, src, dst) in enumerate(
            [
                ("x", x_hbm, x_ref),
                ("tw", tw_hbm, tw),
                ("pairs", pairs_hbm, pairs_ref),
                ("dft", dft_hbm, dft),
                ("edges", edges_hbm, edges_ref),
                ("counts", counts_hbm, counts_ref),
                ("tab", tab_hbm, tab),
                ("obs", obs_hbm, obs),
                ("tabt", tabt_hbm, tabt),
                ("idft", idft_hbm, idft),
            ]
        )
    }
    for load in loads.values():
        load.start()

    loads["x"].wait()
    values = x_ref[...].astype(jnp.float32)
    centred = values - jnp.mean(values, axis=1, keepdims=True)
    spread = jnp.sqrt(jnp.mean(centred * centred, axis=1, keepdims=True) + EPSILON)
    nf[...] = centred / spread

    loads["tw"].wait()
    for r in range(CHAN // 16):
        rows = slice(16 * r, 16 * r + 16)
        for h in range(N2 // 128):
            lanes = slice(128 * h, 128 * h + 128)
            a = [
                nf[rows, N2 * t + 128 * h : N2 * t + 128 * h + 128].astype(jnp.bfloat16).astype(jnp.float32)
                for t in range(N1)
            ]
            y = forward16(a)
            for f in range(N1):
                yr, yi = y[f] if f <= 8 else y[16 - f]
                c = tw[f, 0:1, lanes]
                s = tw[f, 1:2, lanes]
                if yi is None:
                    zr, zi = yr * c, -(yr * s)
                elif f <= 8:
                    zr, zi = yr * c + yi * s, yi * c - yr * s
                else:
                    zr, zi = yr * c - yi * s, -(yi * c) - yr * s
                z[32 * f + 16 * r : 32 * f + 16 * r + 16, lanes] = zr.astype(jnp.bfloat16)
                z[32 * f + 16 * r : 32 * f + 16 * r + 16, N2 + 128 * h : N2 + 128 * h + 128] = zi.astype(jnp.bfloat16)

    def spec_copy(g, hop):
        part = pl.ds(g * PER, PER)
        return pltpu.make_async_remote_copy(
            src_ref=reach.at[part, pl.ds(0, CHAN)],
            dst_ref=reach.at[part, pl.ds(CHAN * hop, CHAN)],
            send_sem=s_sem.at[hop - 1, g],
            recv_sem=r_sem.at[hop - 1, g],
            device_id=at(hop),
            device_id_type=MESH,
        )

    def grad_copy(g, hop):
        part = pl.ds(g * PER, PER)
        return pltpu.make_async_remote_copy(
            src_ref=psend.at[hop - 1, part],
            dst_ref=precv.at[hop - 1, part],
            send_sem=bs_sem.at[hop - 1, g],
            recv_sem=br_sem.at[hop - 1, g],
            device_id=at(-hop),
            device_id_type=MESH,
        )

    loads["dft"].wait()
    pl.semaphore_wait(barrier, 5)
    for g in range(CHUNKS):
        rows = PER * CHAN
        s = jnp.dot(z[rows * g : rows * (g + 1)], dft[...], preferred_element_type=jnp.float32)
        s = (s * (1.0 / math.sqrt(SAMPLES))).astype(jnp.bfloat16)
        reach[PER * g : PER * (g + 1), 0:CHAN, :] = s.reshape(PER, CHAN, 2 * F2)
        spec_copy(g, 1).start()
        spec_copy(g, 2).start()

    loads["pairs"].wait()
    chan_ids = lax.broadcasted_iota(jnp.int32, (128, PAIRS), 0)
    hits1 = (chan_ids == pairs_ref[0:1, :]).astype(jnp.float32)
    hits2 = (chan_ids == pairs_ref[1:2, :]).astype(jnp.float32)
    scatter = jnp.concatenate([hits1, hits2], axis=1).astype(jnp.bfloat16)[: 3 * CHAN]
    gather = jnp.concatenate([hits1.T, hits2.T], axis=0).astype(jnp.bfloat16)[:, : 3 * CHAN]

    lane_bins = lax.broadcasted_iota(jnp.int32, (1, F2), 1) * N1

    def insides(f1):
        bins = lane_bins + f1
        return [(bins >= edges_ref[n]) & (bins < edges_ref[n + 1]) for n in range(BANDS)]

    loads["edges"].wait()
    loads["tab"].wait()
    corr[...] = jnp.zeros_like(corr)

    def correlate(g, carry):
        spec_copy(g, 1).wait_recv()
        spec_copy(g, 2).wait_recv()
        for i in range(PER):
            f1 = g * PER + i
            both = jnp.dot(gather, reach[f1], preferred_element_type=jnp.float32)
            ab[f1] = both.astype(jnp.bfloat16)
            ar, ai = both[:PAIRS, :F2], both[:PAIRS, F2:]
            br, bi = both[PAIRS:, :F2], both[PAIRS:, F2:]
            xr = ar * br + ai * bi
            xi = ai * br - ar * bi
            for n, inside in enumerate(insides(f1)):
                rows = slice(PAIRS * n, PAIRS * (n + 1))
                xm[rows, 2 * F2 * i : 2 * F2 * i + F2] = jnp.where(inside, xr, 0.0).astype(jnp.bfloat16)
                xm[rows, 2 * F2 * i + F2 : 2 * F2 * (i + 1)] = jnp.where(inside, xi, 0.0).astype(jnp.bfloat16)
        part = tab[pl.ds(g * PER, PER)].reshape(PER * 2 * F2, LAGS)
        corr[...] += jnp.dot(xm[...], part, preferred_element_type=jnp.float32)
        return carry

    lax.fori_loop(0, CHUNKS, correlate, 0)

    loads["obs"].wait()
    loads["counts"].wait()
    slot = lax.broadcasted_iota(jnp.int32, (PAIRS, 1), 0)
    live = (slot < counts_ref[0]).astype(jnp.float32)
    squares = jnp.zeros((PAIRS, 1), jnp.float32)
    for n in range(BANDS):
        rows = slice(PAIRS * n, PAIRS * (n + 1))
        residual = (corr[rows] - obs[n]) * live
        squares = squares + jnp.sum(residual * residual, axis=1, keepdims=True)
        wgt[rows] = (residual * (1.0 / math.sqrt(FREQ_BINS / 8.0))).astype(jnp.bfloat16)
    misfit = squares * (0.5 / (BANDS * LAGS))
    mis_ref[...] = jnp.broadcast_to(misfit, (PAIRS, PAIRS)).T[0:1]

    loads["tabt"].wait()

    def spread_back(g, carry):
        raw[...] = jnp.dot(wgt[...], tabt[g], preferred_element_type=jnp.float32)
        for i in range(PER):
            f1 = g * PER + i
            cols = slice(2 * F2 * i, 2 * F2 * (i + 1))
            ins = [jnp.concatenate([m, m], axis=1) for m in insides(f1)]
            grad = jnp.where(ins[0], raw[0:PAIRS, cols], 0.0)
            grad = jnp.where(ins[1], raw[PAIRS : 2 * PAIRS, cols], grad)
            grad = jnp.where(ins[2], raw[2 * PAIRS :, cols], grad)
            gr, gi = grad[:, :F2], grad[:, F2:]
            both = ab[f1].astype(jnp.float32)
            ar, ai = both[:PAIRS, :F2], both[:PAIRS, F2:]
            br, bi = both[PAIRS:, :F2], both[PAIRS:, F2:]
            first = jnp.concatenate([gr * br - gi * bi, gr * bi + gi * br], axis=1)
            second = jnp.concatenate([gr * ar + gi * ai, gr * ai - gi * ar], axis=1)
            grads = jnp.concatenate([first, second], axis=0).astype(jnp.bfloat16)
            sums = jnp.dot(scatter, grads, preferred_element_type=jnp.float32)
            own[f1] = sums[:CHAN]
            psend[0, f1] = sums[CHAN : 2 * CHAN].astype(jnp.bfloat16)
            psend[1, f1] = sums[2 * CHAN :].astype(jnp.bfloat16)
        grad_copy(g, 1).start()
        grad_copy(g, 2).start()
        return carry

    lax.fori_loop(0, CHUNKS, spread_back, 0)

    loads["idft"].wait()

    def invert(g, carry):
        grad_copy(g, 1).wait_recv()
        grad_copy(g, 2).wait_recv()
        part = pl.ds(g * PER, PER)
        total = own[part] + precv[0, part].astype(jnp.float32) + precv[1, part].astype(jnp.float32)
        coeffs = total.astype(jnp.bfloat16).reshape(PER * CHAN, 2 * F2)
        u = jnp.dot(coeffs, idft[...], preferred_element_type=jnp.float32)
        for i in range(PER):
            f1 = g * PER + i
            ur, ui = u[CHAN * i : CHAN * (i + 1), :N2], u[CHAN * i : CHAN * (i + 1), N2:]
            c, s = tw[f1, 0:1], tw[f1, 1:2]
            v[f1, 0] = ur * c - ui * s
            v[f1, 1] = ur * s + ui * c
        return carry

    lax.fori_loop(0, CHUNKS, invert, 0)

    sign = (1 - 2 * band).astype(jnp.float32)
    half = N1 // 2 * N2
    for r in range(CHAN // 16):
        rows = slice(16 * r, 16 * r + 16)
        total_e = jnp.zeros((16, 128), jnp.float32)
        total_w = jnp.zeros((16, 128), jnp.float32)
        for h in range(N2 // 128):
            lanes = slice(128 * h, 128 * h + 128)
            vr = [v[f, 0, rows, lanes] for f in range(N1)]
            vi = [v[f, 1, rows, lanes] for f in range(N1)]
            even, odd = inverse16(vr, vi)
            for t in range(8):
                lo = N2 * t + 128 * h
                out = slice(lo, lo + 128)
                total_e = total_e + even[t]
                low, high = nf[rows, out], nf[rows, half + lo : half + lo + 128]
                total_w = total_w + (even[t] * (low + high) + odd[t] * (low - high))
                mine = odd[t] * sign
                field[rows, out] = even[t] + mine
                fsend[rows, out] = (even[t] - mine).astype(jnp.bfloat16)
        sum_u = jnp.sum(total_e, axis=1, keepdims=True) * (2.0 / SAMPLES)
        sum_w = jnp.sum(total_w, axis=1, keepdims=True) * (1.0 / SAMPLES)
        ssend[rows, 0:128] = jnp.broadcast_to(sum_u, (16, 128))
        ssend[rows, 128:256] = jnp.broadcast_to(sum_w, (16, 128))

    swaps = [
        pltpu.make_async_remote_copy(
            src_ref=src, dst_ref=dst, send_sem=x_ssem.at[i], recv_sem=x_rsem.at[i],
            device_id=partner, device_id_type=MESH,
        )
        for i, (src, dst) in enumerate([(ssend, srecv), (fsend, frecv)])
    ]
    for swap in swaps:
        swap.start()
    for swap in swaps:
        swap.wait()
    mean_u = ssend[:, 0:1] + srecv[:, 0:1]
    mean_w = ssend[:, 128:129] + srecv[:, 128:129]
    mine = nf[:, pl.ds(pl.multiple_of(band * half, half), half)]
    adj_ref[...] = (field[...] + frecv[...].astype(jnp.float32) - mean_u - mine * mean_w) / spread

    def drain(g, carry):
        for hop in (1, 2):
            spec_copy(g, hop).wait_send()
            grad_copy(g, hop).wait_send()
        return carry

    lax.fori_loop(0, CHUNKS, drain, 0)


def per_device(traces, pair_list, counts, band_edges, observed):
    bf16, f32 = jnp.bfloat16, jnp.float32
    table = lag_table()
    dft = dft_table()
    tables = [
        jnp.asarray(table),
        jnp.asarray(np.ascontiguousarray(np.swapaxes(table.reshape(CHUNKS, PER * 2 * F2, LAGS), 1, 2))),
        jnp.asarray(dft.astype(ml_dtypes.bfloat16)),
        jnp.asarray((dft.T / math.sqrt(SAMPLES)).astype(ml_dtypes.bfloat16)),
        jnp.asarray(twiddles()),
    ]
    vmem = pl.BlockSpec(memory_space=pltpu.VMEM)
    hbm = pl.BlockSpec(memory_space=pltpu.HBM)
    dma = pltpu.SemaphoreType.DMA
    adjoint, misfit = pl.pallas_call(
        kernel,
        out_shape=(
            jax.ShapeDtypeStruct((CHAN, SAMPLES // 2), f32),
            jax.ShapeDtypeStruct((1, PAIRS), f32),
        ),
        in_specs=[hbm] * 10,
        out_specs=(vmem, vmem),
        scratch_shapes=[
            pltpu.VMEM((CHAN, SAMPLES), bf16),
            pltpu.VMEM((2, PAIRS), jnp.int32),
            pltpu.SMEM((1,), jnp.int32),
            pltpu.SMEM((BANDS + 1,), jnp.int32),
            pltpu.VMEM((N1, 2 * F2, LAGS), bf16),
            pltpu.VMEM((CHUNKS, LAGS, PER * 2 * F2), bf16),
            pltpu.VMEM((2 * N2, 2 * F2), bf16),
            pltpu.VMEM((2 * F2, 2 * N2), bf16),
            pltpu.VMEM((N1, 2, N2), f32),
            pltpu.VMEM((BANDS, PAIRS, LAGS), f32),
            pltpu.VMEM((CHAN, SAMPLES), f32),
            pltpu.VMEM((N1 * CHAN, 2 * N2), bf16),
            pltpu.VMEM((N1, 3 * CHAN, 2 * F2), bf16),
            pltpu.VMEM((N1, 2 * PAIRS, 2 * F2), bf16),
            pltpu.VMEM((BANDS * PAIRS, PER * 2 * F2), bf16),
            pltpu.VMEM((BANDS * PAIRS, LAGS), f32),
            pltpu.VMEM((BANDS * PAIRS, LAGS), bf16),
            pltpu.VMEM((BANDS * PAIRS, PER * 2 * F2), f32),
            pltpu.VMEM((N1, CHAN, 2 * F2), f32),
            pltpu.VMEM((2, N1, CHAN, 2 * F2), bf16),
            pltpu.VMEM((2, N1, CHAN, 2 * F2), bf16),
            pltpu.VMEM((N1, 2, CHAN, N2), f32),
            pltpu.VMEM((CHAN, SAMPLES // 2), f32),
            pltpu.VMEM((CHAN, SAMPLES // 2), bf16),
            pltpu.VMEM((CHAN, SAMPLES // 2), bf16),
            pltpu.VMEM((CHAN, 256), f32),
            pltpu.VMEM((CHAN, 256), f32),
            dma((10,)),
            dma((2, CHUNKS)),
            dma((2, CHUNKS)),
            dma((2, CHUNKS)),
            dma((2, CHUNKS)),
            dma((2,)),
            dma((2,)),
        ],
        compiler_params=pltpu.CompilerParams(
            collective_id=0, has_side_effects=True, vmem_limit_bytes=60 << 20
        ),
        name="misfit_adjoint",
    )(traces, pair_list.T, counts, band_edges, jnp.transpose(observed, (1, 0, 2)), *tables)
    return adjoint, misfit.reshape(PAIRS)


def solution(mesh):
    in_specs = (
        P("blk", None),
        P(("blk", "band"), None),
        P(("blk", "band")),
        P(),
        P(("blk", "band"), None, None),
    )
    out_specs = (P("blk", "band"), P(("blk", "band")))
    return jax.shard_map(
        per_device, mesh=mesh, in_specs=in_specs, out_specs=out_specs, check_vma=False
    )
```

```python
import functools
import math

import jax
import jax.numpy as jnp
import ml_dtypes
import numpy as np
from jax import lax
from jax.experimental import pallas as pl
from jax.experimental.pallas import tpu as pltpu
from jax.sharding import PartitionSpec as P

SAMPLES = 4096
FREQ_BINS = 2048
MAX_LAG = 256
LAGS = 2 * MAX_LAG
BANDS = 3
CHAN = 32
PAIRS = 128
EPSILON = 1e-05
N1 = 16
N2 = 256
F2 = FREQ_BINS // N1
CHUNKS = 4
PER = N1 // CHUNKS
MESH = pl.DeviceIdType.MESH


def lag_table():
    f = np.arange(N1)[:, None] + N1 * np.arange(F2)[None, :]
    shift = np.arange(-MAX_LAG, MAX_LAG)
    angle = np.mod(f[:, :, None] * shift, SAMPLES) * (2.0 * np.pi / SAMPLES)
    rows = np.stack([np.cos(angle), -np.sin(angle)], axis=1) / math.sqrt(FREQ_BINS / 8.0)
    return rows.reshape(N1, 2 * F2, LAGS).astype(ml_dtypes.bfloat16)


def dft_table():
    angle = np.mod(np.arange(N2)[:, None] * np.arange(F2)[None, :], N2) * (2.0 * np.pi / N2)
    c, s = np.cos(angle), np.sin(angle)
    return np.block([[c, -s], [s, c]])


def twiddles():
    angle = np.arange(N1)[:, None] * np.arange(N2)[None, :] * (2.0 * np.pi / SAMPLES)
    return np.stack([np.cos(angle), np.sin(angle)], axis=1).astype(np.float32)


def combine(terms):
    total = None
    for gain, value in terms:
        if abs(gain) < 1e-9:
            continue
        if abs(abs(gain) - 1.0) < 1e-9:
            if total is None:
                total = value if gain > 0 else -value
            else:
                total = total + value if gain > 0 else total - value
        else:
            scaled = value * np.float32(gain)
            total = scaled if total is None else total + scaled
    return total


def cosine(k):
    return math.cos(2.0 * math.pi * k / 16)


def sine(k):
    return math.sin(2.0 * math.pi * k / 16)


def forward16(a):
    s = [a[j] + a[j + 8] for j in range(8)]
    d = [a[j] - a[j + 8] for j in range(8)]
    out = [None] * 9
    p = [None] + [d[j] - d[8 - j] for j in range(1, 4)]
    q = [None] + [d[j] + d[8 - j] for j in range(1, 4)]
    for f in (1, 3, 5, 7):
        real = combine([(1.0, d[0])] + [(cosine(j * f), p[j]) for j in range(1, 4)])
        imag = combine([(-sine(4 * f), d[4])] + [(-sine(j * f), q[j]) for j in range(1, 4)])
        out[f] = (real, imag)
    s2 = [s[j] + s[j + 4] for j in range(4)]
    d2 = [s[j] - s[j + 4] for j in range(4)]
    for f in (2, 6):
        real = combine([(1.0, d2[0]), (cosine(f), d2[1] - d2[3])])
        imag = combine([(-sine(2 * f), d2[2]), (-sine(f), d2[1] + d2[3])])
        out[f] = (real, imag)
    out[4] = (s2[0] - s2[2], s2[3] - s2[1])
    even, odd = s2[0] + s2[2], s2[1] + s2[3]
    out[0] = (even + odd, None)
    out[8] = (even - odd, None)
    return out


def inverse16(vr, vi):
    qr = [vr[0]] + [vr[f] + vr[16 - f] for f in range(1, 8)] + [vr[8]]
    qi = [None] + [vi[f] - vi[16 - f] for f in range(1, 8)]
    even, odd = [None] * 8, [None] * 8
    for t in range(5):
        ce = combine([(cosine(t * f), qr[f]) for f in (0, 2, 4, 6, 8)])
        se = combine([(sine(t * f), qi[f]) for f in (2, 4, 6)])
        co = combine([(cosine(t * f), qr[f]) for f in (1, 3, 5, 7)])
        so = combine([(sine(t * f), qi[f]) for f in (1, 3, 5, 7)])
        even[t] = ce if se is None else ce - se
        if co is None:
            odd[t] = -so
        else:
            odd[t] = co if so is None else co - so
        if 1 <= t <= 3:
            even[8 - t] = ce + se
            odd[8 - t] = -co - so
    return even, odd


def kernel(
    x_hbm, pairs_hbm, counts_hbm, edges_hbm, obs_hbm, tab_hbm, tabt_hbm, dft_hbm, idft_hbm, tw_hbm,
    adj_ref, mis_ref,
    x_ref, pairs_ref, counts_ref, edges_ref, tab, tabt, dft, idft, tw, obs, nf, z, reach, ab, xm, corr, wgt, raw, own, far, nsend, nrecv, fsend, frecv,
    csend, crecv, v, field,
    load_sem, fs_sem, fr_sem, ns_sem, nr_sem, bns_sem, bnr_sem, bfs_sem, bfr_sem, xs_sem, xr_sem,
):
    blk = lax.axis_index("blk")
    band = lax.axis_index("band")
    n_blk = lax.axis_size("blk")

    def at(step):
        return (lax.rem(blk + step + n_blk, n_blk), band)

    odd = lax.rem(blk, 2)
    mate = (blk + 1 - 2 * odd, band)
    partner = (blk, 1 - band)
    barrier = pltpu.get_barrier_semaphore()
    for where in (at(2), at(-2), mate, partner):
        pl.semaphore_signal(barrier, inc=1, device_id=where, device_id_type=MESH)

    loads = {
        name: pltpu.make_async_copy(src, dst, load_sem.at[i])
        for i, (name, src, dst) in enumerate(
            [
                ("x", x_hbm, x_ref),
                ("tw", tw_hbm, tw),
                ("pairs", pairs_hbm, pairs_ref),
                ("dft", dft_hbm, dft),
                ("edges", edges_hbm, edges_ref),
                ("counts", counts_hbm, counts_ref),
                ("tab", tab_hbm, tab),
                ("obs", obs_hbm, obs),
                ("tabt", tabt_hbm, tabt),
                ("idft", idft_hbm, idft),
            ]
        )
    }
    for load in loads.values():
        load.start()

    loads["x"].wait()
    values = x_ref[...].astype(jnp.float32)
    centred = values - jnp.mean(values, axis=1, keepdims=True)
    spread = jnp.sqrt(jnp.mean(centred * centred, axis=1, keepdims=True) + EPSILON)
    gain = 1.0 / spread
    nf[...] = centred * gain

    loads["tw"].wait()
    for r in range(CHAN // 16):
        rows = slice(16 * r, 16 * r + 16)
        for h in range(N2 // 128):
            lanes = slice(128 * h, 128 * h + 128)
            a = [
                nf[rows, N2 * t + 128 * h : N2 * t + 128 * h + 128].astype(jnp.bfloat16).astype(jnp.float32)
                for t in range(N1)
            ]
            y = forward16(a)
            for f in range(N1):
                yr, yi = y[f] if f <= 8 else y[16 - f]
                c = tw[f, 0:1, lanes]
                s = tw[f, 1:2, lanes]
                if yi is None:
                    zr, zi = yr * c, -(yr * s)
                elif f <= 8:
                    zr, zi = yr * c + yi * s, yi * c - yr * s
                else:
                    zr, zi = yr * c - yi * s, -(yi * c) - yr * s
                z[32 * f + 16 * r : 32 * f + 16 * r + 16, lanes] = zr.astype(jnp.bfloat16)
                z[32 * f + 16 * r : 32 * f + 16 * r + 16, N2 + 128 * h : N2 + 128 * h + 128] = zi.astype(jnp.bfloat16)

    def remote(src, dst, sems, slot, where):
        return pltpu.make_async_remote_copy(
            src_ref=src,
            dst_ref=dst,
            send_sem=sems[0].at[slot],
            recv_sem=sems[1].at[slot],
            device_id=where,
            device_id_type=MESH,
        )

    def chunk(g):
        return pl.ds(g * PER, PER)

    def far_spec(g):
        src, dst = reach.at[chunk(g), pl.ds(0, CHAN)], reach.at[chunk(g), pl.ds(2 * CHAN, CHAN)]
        return remote(src, dst, (fs_sem, fr_sem), g, at(2))

    def near_spec(g):
        lo = pl.multiple_of(odd * 2 * CHAN, CHAN)
        src, dst = reach.at[chunk(g), pl.ds(lo, CHAN)], reach.at[chunk(g), pl.ds(CHAN, CHAN)]
        return remote(src, dst, (ns_sem, nr_sem), g, mate)

    def near_grad(g):
        return remote(nsend.at[chunk(g)], nrecv.at[chunk(g)], (bns_sem, bnr_sem), g, mate)

    def far_grad(g):
        return remote(fsend.at[chunk(g)], frecv.at[chunk(g)], (bfs_sem, bfr_sem), g, at(-2))

    def swap(g):
        return remote(csend.at[chunk(g)], crecv.at[chunk(g)], (xs_sem, xr_sem), g, partner)

    loads["dft"].wait()
    pl.semaphore_wait(barrier, 4)
    for g in range(CHUNKS):
        rows = PER * CHAN
        s = jnp.dot(z[rows * g : rows * (g + 1)], dft[...], preferred_element_type=jnp.float32)
        s = (s * (1.0 / math.sqrt(SAMPLES))).astype(jnp.bfloat16)
        reach[PER * g : PER * (g + 1), 0:CHAN, :] = s.reshape(PER, CHAN, 2 * F2)
        far_spec(g).start()

        @pl.when(odd == 0)
        def _():
            near_spec(g).start()


    loads["pairs"].wait()
    chan_ids = lax.broadcasted_iota(jnp.int32, (128, PAIRS), 0)
    hits1 = (chan_ids == pairs_ref[0:1, :]).astype(jnp.float32)
    hits2 = (chan_ids == pairs_ref[1:2, :]).astype(jnp.float32)
    scatter = jnp.concatenate([hits1, hits2], axis=1).astype(jnp.bfloat16)[: 3 * CHAN]
    gather = jnp.concatenate([hits1.T, hits2.T], axis=0).astype(jnp.bfloat16)[:, : 3 * CHAN]

    lane_bins = lax.broadcasted_iota(jnp.int32, (1, F2), 1) * N1

    def insides(f1):
        bins = lane_bins + f1
        return [(bins >= edges_ref[n]) & (bins < edges_ref[n + 1]) for n in range(BANDS)]

    loads["edges"].wait()
    loads["tab"].wait()
    corr[...] = jnp.zeros_like(corr)

    def correlate(g, carry):
        far_spec(g).wait_recv()

        @pl.when(odd == 1)
        def _():
            near_spec(g).start()

        near_spec(g).wait_recv()
        for i in range(PER):
            f1 = g * PER + i
            both = jnp.dot(gather, reach[f1], preferred_element_type=jnp.float32)
            ab[f1] = both.astype(jnp.bfloat16)
            ar, ai = both[:PAIRS, :F2], both[:PAIRS, F2:]
            br, bi = both[PAIRS:, :F2], both[PAIRS:, F2:]
            xr = ar * br + ai * bi
            xi = ai * br - ar * bi
            for n, inside in enumerate(insides(f1)):
                rows = slice(PAIRS * n, PAIRS * (n + 1))
                xm[rows, 2 * F2 * i : 2 * F2 * i + F2] = jnp.where(inside, xr, 0.0).astype(jnp.bfloat16)
                xm[rows, 2 * F2 * i + F2 : 2 * F2 * (i + 1)] = jnp.where(inside, xi, 0.0).astype(jnp.bfloat16)
        part = tab[pl.ds(g * PER, PER)].reshape(PER * 2 * F2, LAGS)
        corr[...] += jnp.dot(xm[...], part, preferred_element_type=jnp.float32)
        return carry

    lax.fori_loop(0, CHUNKS, correlate, 0)

    loads["obs"].wait()
    loads["counts"].wait()
    slot = lax.broadcasted_iota(jnp.int32, (PAIRS, 1), 0)
    live = (slot < counts_ref[0]).astype(jnp.float32)
    squares = jnp.zeros((PAIRS, 1), jnp.float32)
    for n in range(BANDS):
        rows = slice(PAIRS * n, PAIRS * (n + 1))
        residual = (corr[rows] - obs[n]) * live
        squares = squares + jnp.sum(residual * residual, axis=1, keepdims=True)
        wgt[rows] = (residual * (1.0 / math.sqrt(FREQ_BINS / 8.0))).astype(jnp.bfloat16)
    misfit = squares * (0.5 / (BANDS * LAGS))
    mis_ref[...] = jnp.broadcast_to(misfit, (PAIRS, PAIRS)).T[0:1]

    loads["tabt"].wait()

    def spread_back(g, carry):
        raw[...] = jnp.dot(wgt[...], tabt[g], preferred_element_type=jnp.float32)
        for i in range(PER):
            f1 = g * PER + i
            cols = slice(2 * F2 * i, 2 * F2 * (i + 1))
            ins = [jnp.concatenate([m, m], axis=1) for m in insides(f1)]
            grad = jnp.where(ins[0], raw[0:PAIRS, cols], 0.0)
            grad = jnp.where(ins[1], raw[PAIRS : 2 * PAIRS, cols], grad)
            grad = jnp.where(ins[2], raw[2 * PAIRS :, cols], grad)
            gr, gi = grad[:, :F2], grad[:, F2:]
            both = ab[f1].astype(jnp.float32)
            ar, ai = both[:PAIRS, :F2], both[:PAIRS, F2:]
            br, bi = both[PAIRS:, :F2], both[PAIRS:, F2:]
            first = jnp.concatenate([gr * br - gi * bi, gr * bi + gi * br], axis=1)
            second = jnp.concatenate([gr * ar + gi * ai, gr * ai - gi * ar], axis=1)
            grads = jnp.concatenate([first, second], axis=0).astype(jnp.bfloat16)
            sums = jnp.dot(scatter, grads, preferred_element_type=jnp.float32)
            own[f1] = sums[:CHAN]
            nsend[f1] = sums[CHAN : 2 * CHAN].astype(jnp.bfloat16)
            far[f1] = sums[2 * CHAN :]
        near_grad(g).start()

        @pl.when(odd == 0)
        def _():
            fsend[chunk(g)] = far[chunk(g)].astype(jnp.bfloat16)
            far_grad(g).start()

        @pl.when((odd == 1) & (g > 0))
        def _():
            pass_on(g - 1)

        return carry

    def pass_on(g):
        near_grad(g).wait_recv()
        fsend[chunk(g)] = (far[chunk(g)] + nrecv[chunk(g)].astype(jnp.float32)).astype(jnp.bfloat16)
        far_grad(g).start()

    lax.fori_loop(0, CHUNKS, spread_back, 0)

    @pl.when(odd == 1)
    def _():
        pass_on(CHUNKS - 1)

    def gather_sums(g, carry):
        far_grad(g).wait_recv()
        total = own[chunk(g)] + frecv[chunk(g)].astype(jnp.float32)
        own[chunk(g)] = total

        @pl.when(odd == 0)
        def _():
            near_grad(g).wait_recv()
            own[chunk(g)] += nrecv[chunk(g)].astype(jnp.float32)

        csend[chunk(g)] = own[chunk(g)].astype(jnp.bfloat16)
        swap(g).start()
        return carry

    lax.fori_loop(0, CHUNKS, gather_sums, 0)

    loads["idft"].wait()

    def invert(g, carry):
        swap(g).wait_recv()
        total = own[chunk(g)] + crecv[chunk(g)].astype(jnp.float32)
        coeffs = total.astype(jnp.bfloat16).reshape(PER * CHAN, 2 * F2)
        u = jnp.dot(coeffs, idft[...], preferred_element_type=jnp.float32)
        for i in range(PER):
            f1 = g * PER + i
            ur, ui = u[CHAN * i : CHAN * (i + 1), :N2], u[CHAN * i : CHAN * (i + 1), N2:]
            c, s = tw[f1, 0:1], tw[f1, 1:2]
            v[f1, 0] = ur * c - ui * s
            v[f1, 1] = ur * s + ui * c
        return carry

    lax.fori_loop(0, CHUNKS, invert, 0)

    sign = (1 - 2 * band).astype(jnp.float32)
    half = N1 // 2 * N2
    for r in range(CHAN // 16):
        rows = slice(16 * r, 16 * r + 16)
        total_e = jnp.zeros((16, 128), jnp.float32)
        total_w = jnp.zeros((16, 128), jnp.float32)
        for h in range(N2 // 128):
            lanes = slice(128 * h, 128 * h + 128)
            vr = [v[f, 0, rows, lanes] for f in range(N1)]
            vi = [v[f, 1, rows, lanes] for f in range(N1)]
            even, odds = inverse16(vr, vi)
            for t in range(8):
                lo = N2 * t + 128 * h
                out = slice(lo, lo + 128)
                total_e = total_e + even[t]
                low, high = nf[rows, out], nf[rows, half + lo : half + lo + 128]
                total_w = total_w + (even[t] * (low + high) + odds[t] * (low - high))
                field[rows, out] = even[t] + odds[t] * sign
        mean_u = jnp.sum(total_e, axis=1, keepdims=True) * (2.0 / SAMPLES)
        mean_w = jnp.sum(total_w, axis=1, keepdims=True) * (1.0 / SAMPLES)
        mine = nf[rows, pl.ds(pl.multiple_of(band * half, half), half)]
        adj_ref[rows] = (field[rows] - mean_u - mine * mean_w) * gain[rows]

    def drain(g, carry):
        for copy in (far_spec, near_spec, near_grad, far_grad, swap):
            copy(g).wait_send()
        return carry

    lax.fori_loop(0, CHUNKS, drain, 0)


def per_device(traces, pair_list, counts, band_edges, observed):
    bf16, f32 = jnp.bfloat16, jnp.float32
    table = lag_table()
    dft = dft_table()
    tables = [
        jnp.asarray(table),
        jnp.asarray(np.ascontiguousarray(np.swapaxes(table.reshape(CHUNKS, PER * 2 * F2, LAGS), 1, 2))),
        jnp.asarray(dft.astype(ml_dtypes.bfloat16)),
        jnp.asarray((dft.T / math.sqrt(SAMPLES)).astype(ml_dtypes.bfloat16)),
        jnp.asarray(twiddles()),
    ]
    vmem = pl.BlockSpec(memory_space=pltpu.VMEM)
    hbm = pl.BlockSpec(memory_space=pltpu.HBM)
    dma = pltpu.SemaphoreType.DMA
    adjoint, misfit = pl.pallas_call(
        kernel,
        out_shape=(
            pltpu.VMEM((CHAN, SAMPLES // 2), f32),
            pltpu.VMEM((1, PAIRS), f32),
        ),
        in_specs=[hbm] * 10,
        out_specs=(vmem, vmem),
        scratch_shapes=[
            pltpu.VMEM((CHAN, SAMPLES), bf16),
            pltpu.VMEM((2, PAIRS), jnp.int32),
            pltpu.SMEM((1,), jnp.int32),
            pltpu.SMEM((BANDS + 1,), jnp.int32),
            pltpu.VMEM((N1, 2 * F2, LAGS), bf16),
            pltpu.VMEM((CHUNKS, LAGS, PER * 2 * F2), bf16),
            pltpu.VMEM((2 * N2, 2 * F2), bf16),
            pltpu.VMEM((2 * F2, 2 * N2), bf16),
            pltpu.VMEM((N1, 2, N2), f32),
            pltpu.VMEM((BANDS, PAIRS, LAGS), f32),
            pltpu.VMEM((CHAN, SAMPLES), f32),
            pltpu.VMEM((N1 * CHAN, 2 * N2), bf16),
            pltpu.VMEM((N1, 3 * CHAN, 2 * F2), bf16),
            pltpu.VMEM((N1, 2 * PAIRS, 2 * F2), bf16),
            pltpu.VMEM((BANDS * PAIRS, PER * 2 * F2), bf16),
            pltpu.VMEM((BANDS * PAIRS, LAGS), f32),
            pltpu.VMEM((BANDS * PAIRS, LAGS), bf16),
            pltpu.VMEM((BANDS * PAIRS, PER * 2 * F2), f32),
            pltpu.VMEM((N1, CHAN, 2 * F2), f32),
            pltpu.VMEM((N1, CHAN, 2 * F2), f32),
            *[pltpu.VMEM((N1, CHAN, 2 * F2), bf16)] * 6,
            pltpu.VMEM((N1, 2, CHAN, N2), f32),
            pltpu.VMEM((CHAN, SAMPLES // 2), f32),
            dma((10,)),
            *[dma((CHUNKS,))] * 10,
        ],
        compiler_params=pltpu.CompilerParams(
            collective_id=0, has_side_effects=True, vmem_limit_bytes=60 << 20
        ),
        name="misfit_adjoint",
    )(traces, pair_list.T, counts, band_edges, jnp.transpose(observed, (1, 0, 2)), *tables)
    return adjoint, misfit.reshape(PAIRS)


def solution(mesh):
    in_specs = (
        P("blk", None),
        P(("blk", "band"), None),
        P(("blk", "band")),
        P(),
        P(("blk", "band"), None, None),
    )
    out_specs = (P("blk", "band"), P(("blk", "band")))
    return jax.shard_map(
        per_device, mesh=mesh, in_specs=in_specs, out_specs=out_specs, check_vma=False
    )
```

```python
import functools
import math

import jax
import jax.numpy as jnp
import ml_dtypes
import numpy as np
from jax import lax
from jax.experimental import pallas as pl
from jax.experimental.pallas import tpu as pltpu
from jax.sharding import PartitionSpec as P

SAMPLES = 4096
FREQ_BINS = 2048
MAX_LAG = 256
LAGS = 2 * MAX_LAG
BANDS = 3
CHAN = 32
PAIRS = 128
EPSILON = 1e-05
N1 = 16
N2 = 256
F2 = FREQ_BINS // N1
PARTS = ((0, 2), (2, 6), (6, 10), (10, 14), (14, 16))
CHUNKS = len(PARTS)
WIDEST = 4
MESH = pl.DeviceIdType.MESH


def lag_table():
    f = np.arange(N1)[:, None] + N1 * np.arange(F2)[None, :]
    shift = np.arange(-MAX_LAG, MAX_LAG)
    angle = np.mod(f[:, :, None] * shift, SAMPLES) * (2.0 * np.pi / SAMPLES)
    rows = np.stack([np.cos(angle), -np.sin(angle)], axis=1) / math.sqrt(FREQ_BINS / 8.0)
    return rows.reshape(N1, 2 * F2, LAGS).astype(ml_dtypes.bfloat16)


def dft_table():
    angle = np.mod(np.arange(N2)[:, None] * np.arange(F2)[None, :], N2) * (2.0 * np.pi / N2)
    c, s = np.cos(angle), np.sin(angle)
    return np.block([[c, -s], [s, c]])


def twiddles():
    angle = np.arange(N1)[:, None] * np.arange(N2)[None, :] * (2.0 * np.pi / SAMPLES)
    return np.stack([np.cos(angle), np.sin(angle)], axis=1).astype(np.float32)


def combine(terms):
    total = None
    for gain, value in terms:
        if abs(gain) < 1e-9:
            continue
        if abs(abs(gain) - 1.0) < 1e-9:
            if total is None:
                total = value if gain > 0 else -value
            else:
                total = total + value if gain > 0 else total - value
        else:
            scaled = value * np.float32(gain)
            total = scaled if total is None else total + scaled
    return total


def cosine(k):
    return math.cos(2.0 * math.pi * k / 16)


def sine(k):
    return math.sin(2.0 * math.pi * k / 16)


def forward16(a):
    s = [a[j] + a[j + 8] for j in range(8)]
    d = [a[j] - a[j + 8] for j in range(8)]
    out = [None] * 9
    p = [None] + [d[j] - d[8 - j] for j in range(1, 4)]
    q = [None] + [d[j] + d[8 - j] for j in range(1, 4)]
    for f in (1, 3, 5, 7):
        real = combine([(1.0, d[0])] + [(cosine(j * f), p[j]) for j in range(1, 4)])
        imag = combine([(-sine(4 * f), d[4])] + [(-sine(j * f), q[j]) for j in range(1, 4)])
        out[f] = (real, imag)
    s2 = [s[j] + s[j + 4] for j in range(4)]
    d2 = [s[j] - s[j + 4] for j in range(4)]
    for f in (2, 6):
        real = combine([(1.0, d2[0]), (cosine(f), d2[1] - d2[3])])
        imag = combine([(-sine(2 * f), d2[2]), (-sine(f), d2[1] + d2[3])])
        out[f] = (real, imag)
    out[4] = (s2[0] - s2[2], s2[3] - s2[1])
    even, odd = s2[0] + s2[2], s2[1] + s2[3]
    out[0] = (even + odd, None)
    out[8] = (even - odd, None)
    return out


def inverse16(vr, vi):
    qr = [vr[0]] + [vr[f] + vr[16 - f] for f in range(1, 8)] + [vr[8]]
    qi = [None] + [vi[f] - vi[16 - f] for f in range(1, 8)]
    even, odd = [None] * 8, [None] * 8
    for t in range(5):
        ce = combine([(cosine(t * f), qr[f]) for f in (0, 2, 4, 6, 8)])
        se = combine([(sine(t * f), qi[f]) for f in (2, 4, 6)])
        co = combine([(cosine(t * f), qr[f]) for f in (1, 3, 5, 7)])
        so = combine([(sine(t * f), qi[f]) for f in (1, 3, 5, 7)])
        even[t] = ce if se is None else ce - se
        if co is None:
            odd[t] = -so
        else:
            odd[t] = co if so is None else co - so
        if 1 <= t <= 3:
            even[8 - t] = ce + se
            odd[8 - t] = -co - so
    return even, odd


def kernel(
    x_hbm, pairs_hbm, counts_hbm, edges_hbm, obs_hbm, tab_hbm, tabt_hbm, dft_hbm, idft_hbm, tw_hbm,
    adj_ref, mis_ref,
    x_ref, pairs_ref, counts_ref, edges_ref, tab, tabt, dft, idft, tw, obs, nf, z, reach, ab, xm, corr, wgt, raw0, raw1, own, far, nsend, nrecv, fsend, frecv,
    csend, crecv, ssend, srecv, v, field,
    load_sem, fs_sem, fr_sem, ns_sem, nr_sem, bns_sem, bnr_sem, bfs_sem, bfr_sem, xs_sem, xr_sem, ms_sem, mr_sem,
):
    blk = lax.axis_index("blk")
    band = lax.axis_index("band")
    n_blk = lax.axis_size("blk")

    def at(step):
        return (lax.rem(blk + step + n_blk, n_blk), band)

    odd = lax.rem(blk, 2)
    mate = (blk + 1 - 2 * odd, band)
    partner = (blk, 1 - band)
    barrier = pltpu.get_barrier_semaphore()
    for where in (at(-2), mate, partner):
        pl.semaphore_signal(barrier, inc=1, device_id=where, device_id_type=MESH)

    loads = {
        name: pltpu.make_async_copy(src, dst, load_sem.at[i])
        for i, (name, src, dst) in enumerate(
            [
                ("x", x_hbm, x_ref),
                ("tw", tw_hbm, tw),
                ("pairs", pairs_hbm, pairs_ref),
                ("dft", dft_hbm, dft),
                ("edges", edges_hbm, edges_ref),
                ("counts", counts_hbm, counts_ref),
                ("tab", tab_hbm, tab),
                ("obs", obs_hbm, obs),
                ("tabt", tabt_hbm, tabt),
                ("idft", idft_hbm, idft),
            ]
        )
    }
    for load in loads.values():
        load.start()

    loads["x"].wait()
    values = x_ref[...].astype(jnp.float32)
    centred = values - jnp.mean(values, axis=1, keepdims=True)
    spread = jnp.sqrt(jnp.mean(centred * centred, axis=1, keepdims=True) + EPSILON)
    gain = 1.0 / spread
    nf[...] = centred * gain

    loads["tw"].wait()
    for r in range(CHAN // 16):
        rows = slice(16 * r, 16 * r + 16)
        for h in range(N2 // 128):
            lanes = slice(128 * h, 128 * h + 128)
            a = [
                nf[rows, N2 * t + 128 * h : N2 * t + 128 * h + 128].astype(jnp.bfloat16).astype(jnp.float32)
                for t in range(N1)
            ]
            y = forward16(a)
            for f in range(N1):
                yr, yi = y[f] if f <= 8 else y[16 - f]
                c = tw[f, 0:1, lanes]
                s = tw[f, 1:2, lanes]
                if yi is None:
                    zr, zi = yr * c, -(yr * s)
                elif f <= 8:
                    zr, zi = yr * c + yi * s, yi * c - yr * s
                else:
                    zr, zi = yr * c - yi * s, -(yi * c) - yr * s
                z[32 * f + 16 * r : 32 * f + 16 * r + 16, lanes] = zr.astype(jnp.bfloat16)
                z[32 * f + 16 * r : 32 * f + 16 * r + 16, N2 + 128 * h : N2 + 128 * h + 128] = zi.astype(jnp.bfloat16)

    def remote(src, dst, sems, slot, where):
        return pltpu.make_async_remote_copy(
            src_ref=src,
            dst_ref=dst,
            send_sem=sems[0].at[slot],
            recv_sem=sems[1].at[slot],
            device_id=where,
            device_id_type=MESH,
        )

    def chunk(g):
        lo, hi = PARTS[g]
        return pl.ds(lo, hi - lo)

    def far_spec(g):
        src, dst = reach.at[chunk(g), pl.ds(0, CHAN)], reach.at[chunk(g), pl.ds(2 * CHAN, CHAN)]
        return remote(src, dst, (fs_sem, fr_sem), g, at(2))

    def near_spec(g):
        lo = pl.multiple_of(odd * 2 * CHAN, CHAN)
        src, dst = reach.at[chunk(g), pl.ds(lo, CHAN)], reach.at[chunk(g), pl.ds(CHAN, CHAN)]
        return remote(src, dst, (ns_sem, nr_sem), g, mate)

    def near_grad(g):
        return remote(nsend.at[chunk(g)], nrecv.at[chunk(g)], (bns_sem, bnr_sem), g, mate)

    def far_grad(g):
        return remote(fsend.at[chunk(g)], frecv.at[chunk(g)], (bfs_sem, bfr_sem), g, at(-2))

    def swap(r):
        rows = pl.ds(16 * r, 16)
        return remote(csend.at[rows], crecv.at[rows], (xs_sem, xr_sem), r, partner)

    def swap_means(r):
        rows = pl.ds(16 * r, 16)
        return remote(ssend.at[rows], srecv.at[rows], (ms_sem, mr_sem), r, partner)

    loads["dft"].wait()
    pl.semaphore_wait(barrier, 3)
    for g, (lo, hi) in enumerate(PARTS):
        s = jnp.dot(z[CHAN * lo : CHAN * hi], dft[...], preferred_element_type=jnp.float32)
        s = (s * (1.0 / math.sqrt(SAMPLES))).astype(jnp.bfloat16)
        reach[lo:hi, 0:CHAN, :] = s.reshape(hi - lo, CHAN, 2 * F2)
        far_spec(g).start()

        @pl.when(odd == 0)
        def _():
            near_spec(g).start()


    loads["pairs"].wait()
    chan_ids = lax.broadcasted_iota(jnp.int32, (128, PAIRS), 0)
    hits1 = (chan_ids == pairs_ref[0:1, :]).astype(jnp.float32)
    hits2 = (chan_ids == pairs_ref[1:2, :]).astype(jnp.float32)
    scatter = jnp.concatenate([hits1, hits2], axis=1).astype(jnp.bfloat16)[: 3 * CHAN]
    gather = jnp.concatenate([hits1.T, hits2.T], axis=0).astype(jnp.bfloat16)[:, : 3 * CHAN]

    lane_bins = lax.broadcasted_iota(jnp.int32, (1, F2), 1) * N1

    def insides(f1):
        bins = lane_bins + f1
        return [(bins >= edges_ref[n]) & (bins < edges_ref[n + 1]) for n in range(BANDS)]

    loads["edges"].wait()
    loads["tab"].wait()
    for g, (lo, hi) in enumerate(PARTS):
        far_spec(g).wait_recv()

        @pl.when(odd == 1)
        def _(g=g):
            near_spec(g).start()

        near_spec(g).wait_recv()
        for f1 in range(lo, hi):
            both = jnp.dot(gather, reach[f1], preferred_element_type=jnp.float32)
            ab[f1] = both
            ar, ai = both[:PAIRS, :F2], both[:PAIRS, F2:]
            br, bi = both[PAIRS:, :F2], both[PAIRS:, F2:]
            xr = ar * br + ai * bi
            xi = ai * br - ar * bi
            col = 2 * F2 * (f1 - lo)
            for n, inside in enumerate(insides(f1)):
                rows = slice(PAIRS * n, PAIRS * (n + 1))
                xm[rows, col : col + F2] = jnp.where(inside, xr, 0.0).astype(jnp.bfloat16)
                xm[rows, col + F2 : col + 2 * F2] = jnp.where(inside, xi, 0.0).astype(jnp.bfloat16)
        width = 2 * F2 * (hi - lo)
        part = tab[lo:hi].reshape(width, LAGS)
        term = jnp.dot(xm[:, :width], part, preferred_element_type=jnp.float32)
        if g == 0:
            corr[...] = term
        else:
            corr[...] += term

    loads["obs"].wait()
    loads["counts"].wait()
    slot = lax.broadcasted_iota(jnp.int32, (PAIRS, 1), 0)
    live = (slot < counts_ref[0]).astype(jnp.float32)
    squares = jnp.zeros((PAIRS, 1), jnp.float32)
    for n in range(BANDS):
        rows = slice(PAIRS * n, PAIRS * (n + 1))
        residual = (corr[rows] - obs[n]) * live
        squares = squares + jnp.sum(residual * residual, axis=1, keepdims=True)
        wgt[rows] = (residual * (1.0 / math.sqrt(FREQ_BINS / 8.0))).astype(jnp.bfloat16)
    misfit = squares * (0.5 / (BANDS * LAGS))
    mis_ref[...] = jnp.broadcast_to(misfit, (PAIRS, PAIRS)).T[0:1]

    loads["tabt"].wait()

    def lag_adjoint(g):
        lo, hi = PARTS[g]
        cols = slice(2 * F2 * lo, 2 * F2 * hi)
        out = (raw0, raw1)[g % 2]
        out[:, : 2 * F2 * (hi - lo)] = jnp.dot(wgt[...], tabt[:, cols], preferred_element_type=jnp.float32)

    def pass_on(g):
        near_grad(g).wait_recv()
        fsend[chunk(g)] = (far[chunk(g)] + nrecv[chunk(g)].astype(jnp.float32)).astype(jnp.bfloat16)
        far_grad(g).start()

    lag_adjoint(0)
    for g, (lo, hi) in enumerate(PARTS):
        if g + 1 < CHUNKS:
            lag_adjoint(g + 1)
        raw = (raw0, raw1)[g % 2]
        for f1 in range(lo, hi):
            ins = [jnp.concatenate([m, m], axis=1) for m in insides(f1)]
            cols = slice(2 * F2 * (f1 - lo), 2 * F2 * (f1 - lo + 1))
            grad = jnp.where(ins[0], raw[0:PAIRS, cols], 0.0)
            grad = jnp.where(ins[1], raw[PAIRS : 2 * PAIRS, cols], grad)
            grad = jnp.where(ins[2], raw[2 * PAIRS :, cols], grad)
            gr, gi = grad[:, :F2], grad[:, F2:]
            ar, ai = ab[f1, :PAIRS, :F2], ab[f1, :PAIRS, F2:]
            br, bi = ab[f1, PAIRS:, :F2], ab[f1, PAIRS:, F2:]
            first = jnp.concatenate([gr * br - gi * bi, gr * bi + gi * br], axis=1)
            second = jnp.concatenate([gr * ar + gi * ai, gr * ai - gi * ar], axis=1)
            grads = jnp.concatenate([first, second], axis=0).astype(jnp.bfloat16)
            sums = jnp.dot(scatter, grads, preferred_element_type=jnp.float32)
            own[f1] = sums[:CHAN]
            nsend[f1] = sums[CHAN : 2 * CHAN].astype(jnp.bfloat16)
            far[f1] = sums[2 * CHAN :]
        near_grad(g).start()

        @pl.when(odd == 0)
        def _(g=g):
            fsend[chunk(g)] = far[chunk(g)].astype(jnp.bfloat16)
            far_grad(g).start()

        if g > 0:

            @pl.when(odd == 1)
            def _(g=g):
                pass_on(g - 1)

    @pl.when(odd == 1)
    def _():
        pass_on(CHUNKS - 1)

    loads["idft"].wait()
    for g, (lo, hi) in enumerate(PARTS):
        far_grad(g).wait_recv()

        @pl.when(odd == 0)
        def _(g=g):
            near_grad(g).wait_recv()
            own[chunk(g)] += nrecv[chunk(g)].astype(jnp.float32)

        total = own[chunk(g)] + frecv[chunk(g)].astype(jnp.float32)
        coeffs = total.astype(jnp.bfloat16).reshape((hi - lo) * CHAN, 2 * F2)
        u = jnp.dot(coeffs, idft[...], preferred_element_type=jnp.float32)
        for f1 in range(lo, hi):
            rows = slice(CHAN * (f1 - lo), CHAN * (f1 - lo + 1))
            ur, ui = u[rows, :N2], u[rows, N2:]
            c, s = tw[f1, 0:1], tw[f1, 1:2]
            v[f1, 0] = ur * c - ui * s
            v[f1, 1] = ur * s + ui * c

    sign = (1 - 2 * band).astype(jnp.float32)
    half = N1 // 2 * N2
    for r in range(CHAN // 16):
        rows = slice(16 * r, 16 * r + 16)
        total_e = jnp.zeros((16, 128), jnp.float32)
        total_w = jnp.zeros((16, 128), jnp.float32)
        for h in range(N2 // 128):
            lanes = slice(128 * h, 128 * h + 128)
            vr = [v[f, 0, rows, lanes] for f in range(N1)]
            vi = [v[f, 1, rows, lanes] for f in range(N1)]
            even, odds = inverse16(vr, vi)
            for t in range(8):
                lo = N2 * t + 128 * h
                out = slice(lo, lo + 128)
                total_e = total_e + even[t]
                low, high = nf[rows, out], nf[rows, half + lo : half + lo + 128]
                total_w = total_w + (even[t] * (low + high) + odds[t] * (low - high))
                mine = odds[t] * sign
                field[rows, out] = even[t] + mine
                csend[rows, out] = (even[t] - mine).astype(jnp.bfloat16)
        mean_u = jnp.sum(total_e, axis=1, keepdims=True) * (2.0 / SAMPLES)
        mean_w = jnp.sum(total_w, axis=1, keepdims=True) * (1.0 / SAMPLES)
        lane = lax.broadcasted_iota(jnp.int32, (16, 128), 1)
        ssend[rows] = jnp.where(lane == 0, mean_u, mean_w)
        swap_means(r).start()
        swap(r).start()

    for r in range(CHAN // 16):
        rows = slice(16 * r, 16 * r + 16)
        swap_means(r).wait_recv()
        means = ssend[rows] + srecv[rows]
        mine = nf[rows, pl.ds(pl.multiple_of(band * half, half), half)]
        partial = field[rows] - means[:, 0:1] - mine * means[:, 1:2]
        swap(r).wait_recv()
        adj_ref[rows] = (partial + crecv[rows].astype(jnp.float32)) * gain[rows]

    for g in range(CHUNKS):
        for copy in (far_spec, near_spec, near_grad, far_grad):
            copy(g).wait_send()
    for r in range(CHAN // 16):
        swap(r).wait_send()
        swap_means(r).wait_send()


def per_device(traces, pair_list, counts, band_edges, observed):
    bf16, f32 = jnp.bfloat16, jnp.float32
    table = lag_table()
    dft = dft_table()
    tables = [
        jnp.asarray(table),
        jnp.asarray(np.ascontiguousarray(table.reshape(N1 * 2 * F2, LAGS).T)),
        jnp.asarray(dft.astype(ml_dtypes.bfloat16)),
        jnp.asarray((dft.T / math.sqrt(SAMPLES)).astype(ml_dtypes.bfloat16)),
        jnp.asarray(twiddles()),
    ]
    vmem = pl.BlockSpec(memory_space=pltpu.VMEM)
    hbm = pl.BlockSpec(memory_space=pltpu.HBM)
    dma = pltpu.SemaphoreType.DMA
    adjoint, misfit = pl.pallas_call(
        kernel,
        out_shape=(
            pltpu.VMEM((CHAN, SAMPLES // 2), f32),
            pltpu.VMEM((1, PAIRS), f32),
        ),
        in_specs=[hbm] * 10,
        out_specs=(vmem, vmem),
        scratch_shapes=[
            pltpu.VMEM((CHAN, SAMPLES), bf16),
            pltpu.VMEM((2, PAIRS), jnp.int32),
            pltpu.SMEM((1,), jnp.int32),
            pltpu.SMEM((BANDS + 1,), jnp.int32),
            pltpu.VMEM((N1, 2 * F2, LAGS), bf16),
            pltpu.VMEM((LAGS, N1 * 2 * F2), bf16),
            pltpu.VMEM((2 * N2, 2 * F2), bf16),
            pltpu.VMEM((2 * F2, 2 * N2), bf16),
            pltpu.VMEM((N1, 2, N2), f32),
            pltpu.VMEM((BANDS, PAIRS, LAGS), f32),
            pltpu.VMEM((CHAN, SAMPLES), f32),
            pltpu.VMEM((N1 * CHAN, 2 * N2), bf16),
            pltpu.VMEM((N1, 3 * CHAN, 2 * F2), bf16),
            pltpu.VMEM((N1, 2 * PAIRS, 2 * F2), f32),
            pltpu.VMEM((BANDS * PAIRS, WIDEST * 2 * F2), bf16),
            pltpu.VMEM((BANDS * PAIRS, LAGS), f32),
            pltpu.VMEM((BANDS * PAIRS, LAGS), bf16),
            pltpu.VMEM((BANDS * PAIRS, WIDEST * 2 * F2), f32),
            pltpu.VMEM((BANDS * PAIRS, WIDEST * 2 * F2), f32),
            pltpu.VMEM((N1, CHAN, 2 * F2), f32),
            pltpu.VMEM((N1, CHAN, 2 * F2), f32),
            *[pltpu.VMEM((N1, CHAN, 2 * F2), bf16)] * 4,
            *[pltpu.VMEM((CHAN, SAMPLES // 2), bf16)] * 2,
            *[pltpu.VMEM((CHAN, 128), f32)] * 2,
            pltpu.VMEM((N1, 2, CHAN, N2), f32),
            pltpu.VMEM((CHAN, SAMPLES // 2), f32),
            dma((10,)),
            *[dma((CHUNKS,))] * 8,
            *[dma((CHAN // 16,))] * 4,
        ],
        compiler_params=pltpu.CompilerParams(
            collective_id=0, has_side_effects=True, vmem_limit_bytes=60 << 20
        ),
        name="misfit_adjoint",
    )(traces, pair_list.T, counts, band_edges, jnp.transpose(observed, (1, 0, 2)), *tables)
    return adjoint, misfit.reshape(PAIRS)


def solution(mesh):
    in_specs = (
        P("blk", None),
        P(("blk", "band"), None),
        P(("blk", "band")),
        P(),
        P(("blk", "band"), None, None),
    )
    out_specs = (P("blk", "band"), P(("blk", "band")))
    return jax.shard_map(
        per_device, mesh=mesh, in_specs=in_specs, out_specs=out_specs, check_vma=False
    )
```

```python
import functools
import math

import jax
import jax.numpy as jnp
import ml_dtypes
import numpy as np
from jax import lax
from jax.experimental import pallas as pl
from jax.experimental.pallas import tpu as pltpu
from jax.sharding import PartitionSpec as P

SAMPLES = 4096
FREQ_BINS = 2048
MAX_LAG = 256
LAGS = 2 * MAX_LAG
BANDS = 3
CHAN = 32
PAIRS = 128
EPSILON = 1e-05
N1 = 16
N2 = 256
F2 = FREQ_BINS // N1
PARTS = ((0, 4), (4, 8), (8, 12), (12, 16))
CHUNKS = len(PARTS)
WIDEST = 4
HALF = CHAN // 2
MESH = pl.DeviceIdType.MESH


def lag_table():
    f = np.arange(N1)[:, None] + N1 * np.arange(F2)[None, :]
    shift = np.arange(-MAX_LAG, MAX_LAG)
    angle = np.mod(f[:, :, None] * shift, SAMPLES) * (2.0 * np.pi / SAMPLES)
    rows = np.stack([np.cos(angle), -np.sin(angle)], axis=1) / math.sqrt(FREQ_BINS / 8.0)
    return rows.reshape(N1, 2 * F2, LAGS).astype(ml_dtypes.bfloat16)


def dft_table():
    angle = np.mod(np.arange(N2)[:, None] * np.arange(F2)[None, :], N2) * (2.0 * np.pi / N2)
    c, s = np.cos(angle), np.sin(angle)
    return np.block([[c, -s], [s, c]])


def twiddles():
    angle = np.arange(N1)[:, None] * np.arange(N2)[None, :] * (2.0 * np.pi / SAMPLES)
    return np.stack([np.cos(angle), np.sin(angle)], axis=1).astype(np.float32)


def combine(terms):
    total = None
    for gain, value in terms:
        if abs(gain) < 1e-9:
            continue
        if abs(abs(gain) - 1.0) < 1e-9:
            if total is None:
                total = value if gain > 0 else -value
            else:
                total = total + value if gain > 0 else total - value
        else:
            scaled = value * np.float32(gain)
            total = scaled if total is None else total + scaled
    return total


def cosine(k):
    return math.cos(2.0 * math.pi * k / 16)


def sine(k):
    return math.sin(2.0 * math.pi * k / 16)


def forward16(a):
    s = [a[j] + a[j + 8] for j in range(8)]
    d = [a[j] - a[j + 8] for j in range(8)]
    out = [None] * 9
    p = [None] + [d[j] - d[8 - j] for j in range(1, 4)]
    q = [None] + [d[j] + d[8 - j] for j in range(1, 4)]
    for f in (1, 3, 5, 7):
        real = combine([(1.0, d[0])] + [(cosine(j * f), p[j]) for j in range(1, 4)])
        imag = combine([(-sine(4 * f), d[4])] + [(-sine(j * f), q[j]) for j in range(1, 4)])
        out[f] = (real, imag)
    s2 = [s[j] + s[j + 4] for j in range(4)]
    d2 = [s[j] - s[j + 4] for j in range(4)]
    for f in (2, 6):
        real = combine([(1.0, d2[0]), (cosine(f), d2[1] - d2[3])])
        imag = combine([(-sine(2 * f), d2[2]), (-sine(f), d2[1] + d2[3])])
        out[f] = (real, imag)
    out[4] = (s2[0] - s2[2], s2[3] - s2[1])
    even, odd = s2[0] + s2[2], s2[1] + s2[3]
    out[0] = (even + odd, None)
    out[8] = (even - odd, None)
    return out


def inverse16(vr, vi):
    qr = [vr[0]] + [vr[f] + vr[16 - f] for f in range(1, 8)] + [vr[8]]
    qi = [None] + [vi[f] - vi[16 - f] for f in range(1, 8)]
    even, odd = [None] * 8, [None] * 8
    for t in range(5):
        ce = combine([(cosine(t * f), qr[f]) for f in (0, 2, 4, 6, 8)])
        se = combine([(sine(t * f), qi[f]) for f in (2, 4, 6)])
        co = combine([(cosine(t * f), qr[f]) for f in (1, 3, 5, 7)])
        so = combine([(sine(t * f), qi[f]) for f in (1, 3, 5, 7)])
        even[t] = ce if se is None else ce - se
        if co is None:
            odd[t] = -so
        else:
            odd[t] = co if so is None else co - so
        if 1 <= t <= 3:
            even[8 - t] = ce + se
            odd[8 - t] = -co - so
    return even, odd


def kernel(
    x_hbm, pairs_hbm, counts_hbm, edges_hbm, obs_hbm, tab_hbm, tabt_hbm, dft_hbm, idft_hbm, tw_hbm,
    adj_ref, mis_ref,
    x_ref, pairs_ref, counts_ref, edges_ref, tab, tabt, dft, idft, tw, obs, nf, z, reach, ab, xm, corr, wgt, raw0, raw1, own, far, nsend, nrecv, fsend, frecv,
    csend, crecv, v, field,
    load_sem, fs_sem, fr_sem, ns_sem, nr_sem, bns_sem, bnr_sem, bfs_sem, bfr_sem, xs_sem, xr_sem, lbs_sem, lbr_sem,
):
    blk = lax.axis_index("blk")
    band = lax.axis_index("band")
    n_blk = lax.axis_size("blk")

    def at(step):
        return (lax.rem(blk + step + n_blk, n_blk), band)

    odd = lax.rem(blk, 2)
    mate = (blk + 1 - 2 * odd, band)
    partner = (blk, 1 - band)
    barrier = pltpu.get_barrier_semaphore()
    for where in (at(-2), mate, partner):
        pl.semaphore_signal(barrier, inc=1, device_id=where, device_id_type=MESH)

    loads = {
        name: pltpu.make_async_copy(src, dst, load_sem.at[i])
        for i, (name, src, dst) in enumerate(
            [
                ("x", x_hbm, x_ref),
                ("tw", tw_hbm, tw),
                ("pairs", pairs_hbm, pairs_ref),
                ("dft", dft_hbm, dft),
                ("edges", edges_hbm, edges_ref),
                ("counts", counts_hbm, counts_ref),
                ("tab", tab_hbm, tab),
                ("obs", obs_hbm, obs),
                ("tabt", tabt_hbm, tabt),
                ("idft", idft_hbm, idft),
            ]
        )
    }
    for load in loads.values():
        load.start()

    loads["x"].wait()
    values = x_ref[...].astype(jnp.float32)
    centred = values - jnp.mean(values, axis=1, keepdims=True)
    spread = jnp.sqrt(jnp.mean(centred * centred, axis=1, keepdims=True) + EPSILON)
    gain = 1.0 / spread
    nf[...] = centred * gain

    loads["tw"].wait()
    def transform16(lo, hi):
        for r in range(CHAN // 16):
            rows = slice(16 * r, 16 * r + 16)
            for h in range(N2 // 128):
                lanes = slice(128 * h, 128 * h + 128)
                a = [
                    nf[rows, N2 * t + 128 * h : N2 * t + 128 * h + 128].astype(jnp.bfloat16).astype(jnp.float32)
                    for t in range(N1)
                ]
                y = forward16(a)
                for f in range(lo, hi):
                    yr, yi = y[f] if f <= 8 else y[16 - f]
                    c = tw[f, 0:1, lanes]
                    s = tw[f, 1:2, lanes]
                    if yi is None:
                        zr, zi = yr * c, -(yr * s)
                    elif f <= 8:
                        zr, zi = yr * c + yi * s, yi * c - yr * s
                    else:
                        zr, zi = yr * c - yi * s, -(yi * c) - yr * s
                    out = slice(32 * f + 16 * r, 32 * f + 16 * r + 16)
                    z[out, lanes] = zr.astype(jnp.bfloat16)
                    z[out, N2 + 128 * h : N2 + 128 * h + 128] = zi.astype(jnp.bfloat16)

    transform16(*PARTS[0])

    def remote(src, dst, sems, slot, where):
        return pltpu.make_async_remote_copy(
            src_ref=src,
            dst_ref=dst,
            send_sem=sems[0].at[slot],
            recv_sem=sems[1].at[slot],
            device_id=where,
            device_id_type=MESH,
        )

    def chunk(g):
        lo, hi = PARTS[g]
        return pl.ds(lo, hi - lo)

    def far_spec(g):
        src, dst = reach.at[chunk(g), pl.ds(0, CHAN)], reach.at[chunk(g), pl.ds(2 * CHAN, CHAN)]
        return remote(src, dst, (fs_sem, fr_sem), g, at(2))

    def near_spec(g):
        lo = pl.multiple_of(odd * 2 * CHAN, CHAN)
        src, dst = reach.at[chunk(g), pl.ds(lo, CHAN)], reach.at[chunk(g), pl.ds(CHAN, CHAN)]
        return remote(src, dst, (ns_sem, nr_sem), g, mate)

    def near_grad(g):
        return remote(nsend.at[chunk(g)], nrecv.at[chunk(g)], (bns_sem, bnr_sem), g, mate)

    def back(crosses):
        return (at(-2)[0], jnp.where(crosses, 1 - band, band))

    def far_grad(g):
        rows = chunk(g), pl.ds(0, HALF)
        return remote(fsend.at[rows], frecv.at[rows], (bfs_sem, bfr_sem), g, back(lax.rem(blk, 16) < 2))

    def late_grad(i):
        rows = pl.ds(i * N1 // 2, N1 // 2), pl.ds(HALF, HALF)
        return remote(fsend.at[rows], frecv.at[rows], (lbs_sem, lbr_sem), i, at(-2))

    def swap(r):
        rows = pl.ds(16 * r, 16)
        return remote(csend.at[rows], crecv.at[rows], (xs_sem, xr_sem), r, partner)

    loads["dft"].wait()
    pl.semaphore_wait(barrier, 3)
    for g, (lo, hi) in enumerate(PARTS):
        if g == 1:
            transform16(lo, N1)
        s = jnp.dot(z[CHAN * lo : CHAN * hi], dft[...], preferred_element_type=jnp.float32)
        s = (s * (1.0 / math.sqrt(SAMPLES))).astype(jnp.bfloat16)
        reach[lo:hi, 0:CHAN, :] = s.reshape(hi - lo, CHAN, 2 * F2)
        far_spec(g).start()

        @pl.when(odd == 0)
        def _():
            near_spec(g).start()


    loads["pairs"].wait()
    chan_ids = lax.broadcasted_iota(jnp.int32, (128, PAIRS), 0)
    hits1 = (chan_ids == pairs_ref[0:1, :]).astype(jnp.float32)
    hits2 = (chan_ids == pairs_ref[1:2, :]).astype(jnp.float32)
    scatter = jnp.concatenate([hits1, hits2], axis=1).astype(jnp.bfloat16)[: 3 * CHAN]
    gather = jnp.concatenate([hits1.T, hits2.T], axis=0).astype(jnp.bfloat16)[:, : 3 * CHAN]

    lane_bins = lax.broadcasted_iota(jnp.int32, (1, F2), 1) * N1

    def insides(f1):
        bins = lane_bins + f1
        return [(bins >= edges_ref[n]) & (bins < edges_ref[n + 1]) for n in range(BANDS)]

    loads["edges"].wait()
    loads["tab"].wait()
    for g, (lo, hi) in enumerate(PARTS):
        far_spec(g).wait_recv()

        @pl.when(odd == 1)
        def _(g=g):
            near_spec(g).start()

        near_spec(g).wait_recv()
        for f1 in range(lo, hi):
            both = jnp.dot(gather, reach[f1], preferred_element_type=jnp.float32)
            ab[f1] = both
            ar, ai = both[:PAIRS, :F2], both[:PAIRS, F2:]
            br, bi = both[PAIRS:, :F2], both[PAIRS:, F2:]
            xr = ar * br + ai * bi
            xi = ai * br - ar * bi
            col = 2 * F2 * (f1 - lo)
            for n, inside in enumerate(insides(f1)):
                rows = slice(PAIRS * n, PAIRS * (n + 1))
                xm[rows, col : col + F2] = jnp.where(inside, xr, 0.0).astype(jnp.bfloat16)
                xm[rows, col + F2 : col + 2 * F2] = jnp.where(inside, xi, 0.0).astype(jnp.bfloat16)
        width = 2 * F2 * (hi - lo)
        part = tab[lo:hi].reshape(width, LAGS)
        term = jnp.dot(xm[:, :width], part, preferred_element_type=jnp.float32)
        if g == 0:
            corr[...] = term
        else:
            corr[...] += term

    loads["obs"].wait()
    loads["counts"].wait()
    slot = lax.broadcasted_iota(jnp.int32, (PAIRS, 1), 0)
    live = (slot < counts_ref[0]).astype(jnp.float32)
    squares = jnp.zeros((PAIRS, 1), jnp.float32)
    for n in range(BANDS):
        rows = slice(PAIRS * n, PAIRS * (n + 1))
        residual = (corr[rows] - obs[n]) * live
        squares = squares + jnp.sum(residual * residual, axis=1, keepdims=True)
        wgt[rows] = (residual * (1.0 / math.sqrt(FREQ_BINS / 8.0))).astype(jnp.bfloat16)
    misfit = squares * (0.5 / (BANDS * LAGS))
    mis_ref[...] = jnp.broadcast_to(misfit, (PAIRS, PAIRS)).T[0:1]

    loads["tabt"].wait()

    def lag_adjoint(g):
        lo, hi = PARTS[g]
        cols = slice(2 * F2 * lo, 2 * F2 * hi)
        out = (raw0, raw1)[g % 2]
        out[:, : 2 * F2 * (hi - lo)] = jnp.dot(wgt[...], tabt[:, cols], preferred_element_type=jnp.float32)

    def pass_on(g):
        near_grad(g).wait_recv()
        fsend[chunk(g)] = (far[chunk(g)] + nrecv[chunk(g)].astype(jnp.float32)).astype(jnp.bfloat16)
        far_grad(g).start()

    lag_adjoint(0)
    for g, (lo, hi) in enumerate(PARTS):
        if 0 < g < CHUNKS - 1:
            lag_adjoint(g + 1)
        raw = (raw0, raw1)[g % 2]
        for f1 in range(lo, hi):
            ins = [jnp.concatenate([m, m], axis=1) for m in insides(f1)]
            cols = slice(2 * F2 * (f1 - lo), 2 * F2 * (f1 - lo + 1))
            grad = jnp.where(ins[0], raw[0:PAIRS, cols], 0.0)
            grad = jnp.where(ins[1], raw[PAIRS : 2 * PAIRS, cols], grad)
            grad = jnp.where(ins[2], raw[2 * PAIRS :, cols], grad)
            gr, gi = grad[:, :F2], grad[:, F2:]
            ar, ai = ab[f1, :PAIRS, :F2], ab[f1, :PAIRS, F2:]
            br, bi = ab[f1, PAIRS:, :F2], ab[f1, PAIRS:, F2:]
            first = jnp.concatenate([gr * br - gi * bi, gr * bi + gi * br], axis=1)
            second = jnp.concatenate([gr * ar + gi * ai, gr * ai - gi * ar], axis=1)
            grads = jnp.concatenate([first, second], axis=0).astype(jnp.bfloat16)
            sums = jnp.dot(scatter, grads, preferred_element_type=jnp.float32)
            own[f1] = sums[:CHAN]
            nsend[f1] = sums[CHAN : 2 * CHAN].astype(jnp.bfloat16)
            far[f1] = sums[2 * CHAN :]
        near_grad(g).start()

        @pl.when(odd == 0)
        def _(g=g):
            fsend[chunk(g)] = far[chunk(g)].astype(jnp.bfloat16)
            far_grad(g).start()

        if g == 0:
            lag_adjoint(1)
        else:

            @pl.when(odd == 1)
            def _(g=g):
                pass_on(g - 1)

    @pl.when(odd == 1)
    def _():
        pass_on(CHUNKS - 1)

    for i in range(2):
        late_grad(i).start()

    loads["idft"].wait()

    @pl.when(odd == 0)
    def _():
        for g in range(CHUNKS):
            near_grad(g).wait_recv()
            own[chunk(g)] += nrecv[chunk(g)].astype(jnp.float32)

    def invert(r, lo, hi):
        rows = slice(HALF * r, HALF * (r + 1))
        total = own[lo:hi, rows] + frecv[lo:hi, rows].astype(jnp.float32)
        coeffs = total.astype(jnp.bfloat16).reshape((hi - lo) * HALF, 2 * F2)
        u = jnp.dot(coeffs, idft[...], preferred_element_type=jnp.float32)
        for f1 in range(lo, hi):
            part = slice(HALF * (f1 - lo), HALF * (f1 - lo + 1))
            ur, ui = u[part, :N2], u[part, N2:]
            c, s = tw[f1, 0:1], tw[f1, 1:2]
            v[f1, 0, rows] = ur * c - ui * s
            v[f1, 1, rows] = ur * s + ui * c

    sign = (1 - 2 * band).astype(jnp.float32)
    half = N1 // 2 * N2
    my_means = []
    for r in range(CHAN // 16):
        rows = slice(16 * r, 16 * r + 16)
        if r == 0:
            for g in range(CHUNKS):
                far_grad(g).wait_recv()
                invert(0, *PARTS[g])
        else:
            for i in range(2):
                late_grad(i).wait_recv()
                invert(1, i * N1 // 2, (i + 1) * N1 // 2)
        total_e = jnp.zeros((16, 128), jnp.float32)
        total_w = jnp.zeros((16, 128), jnp.float32)
        for h in range(N2 // 128):
            lanes = slice(128 * h, 128 * h + 128)
            vr = [v[f, 0, rows, lanes] for f in range(N1)]
            vi = [v[f, 1, rows, lanes] for f in range(N1)]
            even, odds = inverse16(vr, vi)
            for t in range(8):
                lo = N2 * t + 128 * h
                out = slice(lo, lo + 128)
                total_e = total_e + even[t]
                low, high = nf[rows, out], nf[rows, half + lo : half + lo + 128]
                total_w = total_w + (even[t] * (low + high) + odds[t] * (low - high))
                mine = odds[t] * sign
                field[rows, out] = even[t] + mine
                csend[rows, out] = (even[t] - mine).astype(jnp.bfloat16)
        mean_u = jnp.sum(total_e, axis=1, keepdims=True) * (2.0 / SAMPLES)
        mean_w = jnp.sum(total_w, axis=1, keepdims=True) * (1.0 / SAMPLES)
        my_means.append((mean_u, mean_w))
        lane = lax.broadcasted_iota(jnp.int32, (16, 128), 1)
        high_u, high_w = mean_u.astype(jnp.bfloat16).astype(jnp.float32), mean_w.astype(jnp.bfloat16).astype(jnp.float32)
        packed = jnp.where(lane == 0, high_u, jnp.where(lane == 1, mean_u - high_u, high_w))
        packed = jnp.where(lane == 3, mean_w - high_w, packed)
        csend[rows, half:] = packed.astype(jnp.bfloat16)
        swap(r).start()

    for r in range(CHAN // 16):
        rows = slice(16 * r, 16 * r + 16)
        mine = nf[rows, pl.ds(pl.multiple_of(band * half, half), half)]
        swap(r).wait_recv()
        means = crecv[rows, half:].astype(jnp.float32)
        mean_u = my_means[r][0] + (means[:, 0:1] + means[:, 1:2])
        mean_w = my_means[r][1] + (means[:, 2:3] + means[:, 3:4])
        total = field[rows] + crecv[rows, :half].astype(jnp.float32)
        adj_ref[rows] = (total - mean_u - mine * mean_w) * gain[rows]

    for g in range(CHUNKS):
        for copy in (far_spec, near_spec, near_grad, far_grad):
            copy(g).wait_send()
    for i in range(2):
        late_grad(i).wait_send()
    for r in range(CHAN // 16):
        swap(r).wait_send()


def per_device(traces, pair_list, counts, band_edges, observed):
    bf16, f32 = jnp.bfloat16, jnp.float32
    table = lag_table()
    dft = dft_table()
    tables = [
        jnp.asarray(table),
        jnp.asarray(np.ascontiguousarray(table.reshape(N1 * 2 * F2, LAGS).T)),
        jnp.asarray(dft.astype(ml_dtypes.bfloat16)),
        jnp.asarray((dft.T / math.sqrt(SAMPLES)).astype(ml_dtypes.bfloat16)),
        jnp.asarray(twiddles()),
    ]
    vmem = pl.BlockSpec(memory_space=pltpu.VMEM)
    hbm = pl.BlockSpec(memory_space=pltpu.HBM)
    dma = pltpu.SemaphoreType.DMA
    adjoint, misfit = pl.pallas_call(
        kernel,
        out_shape=(
            pltpu.VMEM((CHAN, SAMPLES // 2), f32),
            pltpu.VMEM((1, PAIRS), f32),
        ),
        in_specs=[hbm] * 10,
        out_specs=(vmem, vmem),
        scratch_shapes=[
            pltpu.VMEM((CHAN, SAMPLES), bf16),
            pltpu.VMEM((2, PAIRS), jnp.int32),
            pltpu.SMEM((1,), jnp.int32),
            pltpu.SMEM((BANDS + 1,), jnp.int32),
            pltpu.VMEM((N1, 2 * F2, LAGS), bf16),
            pltpu.VMEM((LAGS, N1 * 2 * F2), bf16),
            pltpu.VMEM((2 * N2, 2 * F2), bf16),
            pltpu.VMEM((2 * F2, 2 * N2), bf16),
            pltpu.VMEM((N1, 2, N2), f32),
            pltpu.VMEM((BANDS, PAIRS, LAGS), f32),
            pltpu.VMEM((CHAN, SAMPLES), f32),
            pltpu.VMEM((N1 * CHAN, 2 * N2), bf16),
            pltpu.VMEM((N1, 3 * CHAN, 2 * F2), bf16),
            pltpu.VMEM((N1, 2 * PAIRS, 2 * F2), f32),
            pltpu.VMEM((BANDS * PAIRS, WIDEST * 2 * F2), bf16),
            pltpu.VMEM((BANDS * PAIRS, LAGS), f32),
            pltpu.VMEM((BANDS * PAIRS, LAGS), bf16),
            pltpu.VMEM((BANDS * PAIRS, WIDEST * 2 * F2), f32),
            pltpu.VMEM((BANDS * PAIRS, WIDEST * 2 * F2), f32),
            pltpu.VMEM((N1, CHAN, 2 * F2), f32),
            pltpu.VMEM((N1, CHAN, 2 * F2), f32),
            *[pltpu.VMEM((N1, CHAN, 2 * F2), bf16)] * 4,
            *[pltpu.VMEM((CHAN, SAMPLES // 2 + 128), bf16)] * 2,
            pltpu.VMEM((N1, 2, CHAN, N2), f32),
            pltpu.VMEM((CHAN, SAMPLES // 2), f32),
            dma((10,)),
            *[dma((CHUNKS,))] * 8,
            *[dma((CHAN // 16,))] * 4,
        ],
        compiler_params=pltpu.CompilerParams(
            collective_id=0, has_side_effects=True, vmem_limit_bytes=60 << 20
        ),
        name="misfit_adjoint",
    )(traces, pair_list.T, counts, band_edges, jnp.transpose(observed, (1, 0, 2)), *tables)
    return adjoint, misfit.reshape(PAIRS)


def solution(mesh):
    in_specs = (
        P("blk", None),
        P(("blk", "band"), None),
        P(("blk", "band")),
        P(),
        P(("blk", "band"), None, None),
    )
    out_specs = (P("blk", "band"), P(("blk", "band")))
    return jax.shard_map(
        per_device, mesh=mesh, in_specs=in_specs, out_specs=out_specs, check_vma=False
    )
```

```python
import functools
import math

import jax
import jax.numpy as jnp
import ml_dtypes
import numpy as np
from jax import lax
from jax.experimental import pallas as pl
from jax.experimental.pallas import tpu as pltpu
from jax.sharding import PartitionSpec as P

SAMPLES = 4096
FREQ_BINS = 2048
MAX_LAG = 256
LAGS = 2 * MAX_LAG
BANDS = 3
CHAN = 32
PAIRS = 128
EPSILON = 1e-05
N1 = 16
N2 = 256
F2 = FREQ_BINS // N1
PARTS = ((0, 4), (4, 8), (8, 12), (12, 16))
CHUNKS = len(PARTS)
WIDEST = 4
HALF = CHAN // 2
MESH = pl.DeviceIdType.MESH


def lag_table():
    f = np.arange(N1)[:, None] + N1 * np.arange(F2)[None, :]
    shift = np.arange(-MAX_LAG, MAX_LAG)
    angle = np.mod(f[:, :, None] * shift, SAMPLES) * (2.0 * np.pi / SAMPLES)
    rows = np.stack([np.cos(angle), -np.sin(angle)], axis=1) / math.sqrt(FREQ_BINS / 8.0)
    return rows.reshape(N1, 2 * F2, LAGS).astype(ml_dtypes.bfloat16)


def dft_table():
    angle = np.mod(np.arange(N2)[:, None] * np.arange(F2)[None, :], N2) * (2.0 * np.pi / N2)
    c, s = np.cos(angle), np.sin(angle)
    return np.block([[c, -s], [s, c]])


def twiddles():
    angle = np.arange(N1)[:, None] * np.arange(N2)[None, :] * (2.0 * np.pi / SAMPLES)
    return np.stack([np.cos(angle), np.sin(angle)], axis=1).astype(np.float32)


def combine(terms):
    total = None
    for gain, value in terms:
        if abs(gain) < 1e-9:
            continue
        if abs(abs(gain) - 1.0) < 1e-9:
            if total is None:
                total = value if gain > 0 else -value
            else:
                total = total + value if gain > 0 else total - value
        else:
            scaled = value * np.float32(gain)
            total = scaled if total is None else total + scaled
    return total


def cosine(k):
    return math.cos(2.0 * math.pi * k / 16)


def sine(k):
    return math.sin(2.0 * math.pi * k / 16)


def forward16(a):
    s = [a[j] + a[j + 8] for j in range(8)]
    d = [a[j] - a[j + 8] for j in range(8)]
    out = [None] * 9
    p = [None] + [d[j] - d[8 - j] for j in range(1, 4)]
    q = [None] + [d[j] + d[8 - j] for j in range(1, 4)]
    for f in (1, 3, 5, 7):
        real = combine([(1.0, d[0])] + [(cosine(j * f), p[j]) for j in range(1, 4)])
        imag = combine([(-sine(4 * f), d[4])] + [(-sine(j * f), q[j]) for j in range(1, 4)])
        out[f] = (real, imag)
    s2 = [s[j] + s[j + 4] for j in range(4)]
    d2 = [s[j] - s[j + 4] for j in range(4)]
    for f in (2, 6):
        real = combine([(1.0, d2[0]), (cosine(f), d2[1] - d2[3])])
        imag = combine([(-sine(2 * f), d2[2]), (-sine(f), d2[1] + d2[3])])
        out[f] = (real, imag)
    out[4] = (s2[0] - s2[2], s2[3] - s2[1])
    even, odd = s2[0] + s2[2], s2[1] + s2[3]
    out[0] = (even + odd, None)
    out[8] = (even - odd, None)
    return out


def inverse16(vr, vi):
    qr = [vr[0]] + [vr[f] + vr[16 - f] for f in range(1, 8)] + [vr[8]]
    qi = [None] + [vi[f] - vi[16 - f] for f in range(1, 8)]
    even, odd = [None] * 8, [None] * 8
    for t in range(5):
        ce = combine([(cosine(t * f), qr[f]) for f in (0, 2, 4, 6, 8)])
        se = combine([(sine(t * f), qi[f]) for f in (2, 4, 6)])
        co = combine([(cosine(t * f), qr[f]) for f in (1, 3, 5, 7)])
        so = combine([(sine(t * f), qi[f]) for f in (1, 3, 5, 7)])
        even[t] = ce if se is None else ce - se
        if co is None:
            odd[t] = -so
        else:
            odd[t] = co if so is None else co - so
        if 1 <= t <= 3:
            even[8 - t] = ce + se
            odd[8 - t] = -co - so
    return even, odd


def kernel(
    x_hbm, pairs_hbm, counts_hbm, edges_hbm, obs_hbm, tab_hbm, tabt_hbm, dft_hbm, idft_hbm, tw_hbm,
    adj_ref, mis_ref,
    x_ref, pairs_ref, counts_ref, edges_ref, tab, tabt, dft, idft, tw, obs, nf, z, reach, ab, xm, corr, wgt, raw0, raw1, own, far, nsend, nrecv, fsend, frecv,
    csend, crecv, v, field,
    load_sem, fs_sem, fr_sem, ns_sem, nr_sem, bns_sem, bnr_sem, bfs_sem, bfr_sem, xs_sem, xr_sem, lbs_sem, lbr_sem,
):
    blk = lax.axis_index("blk")
    band = lax.axis_index("band")
    n_blk = lax.axis_size("blk")

    def at(step):
        return (lax.rem(blk + step + n_blk, n_blk), band)

    odd = lax.rem(blk, 2)
    mate = (blk + 1 - 2 * odd, band)
    partner = (blk, 1 - band)
    barrier = pltpu.get_barrier_semaphore()
    for where in (at(-2), mate, partner):
        pl.semaphore_signal(barrier, inc=1, device_id=where, device_id_type=MESH)

    loads = {
        name: pltpu.make_async_copy(src, dst, load_sem.at[i])
        for i, (name, src, dst) in enumerate(
            [
                ("x", x_hbm, x_ref),
                ("tw", tw_hbm, tw),
                ("pairs", pairs_hbm, pairs_ref),
                ("dft", dft_hbm, dft),
                ("edges", edges_hbm, edges_ref),
                ("counts", counts_hbm, counts_ref),
                ("tab", tab_hbm, tab),
                ("obs", obs_hbm, obs),
                ("tabt", tabt_hbm, tabt),
                ("idft", idft_hbm, idft),
            ]
        )
    }
    for load in loads.values():
        load.start()

    loads["x"].wait()
    values = x_ref[...].astype(jnp.float32)
    centred = values - jnp.mean(values, axis=1, keepdims=True)
    spread = jnp.sqrt(jnp.mean(centred * centred, axis=1, keepdims=True) + EPSILON)
    gain = 1.0 / spread
    nf[...] = centred * gain

    loads["tw"].wait()
    def transform16(lo, hi):
        for r in range(CHAN // 16):
            rows = slice(16 * r, 16 * r + 16)
            for h in range(N2 // 128):
                lanes = slice(128 * h, 128 * h + 128)
                a = [
                    nf[rows, N2 * t + 128 * h : N2 * t + 128 * h + 128].astype(jnp.bfloat16).astype(jnp.float32)
                    for t in range(N1)
                ]
                y = forward16(a)
                for f in range(lo, hi):
                    yr, yi = y[f] if f <= 8 else y[16 - f]
                    c = tw[f, 0:1, lanes]
                    s = tw[f, 1:2, lanes]
                    if yi is None:
                        zr, zi = yr * c, -(yr * s)
                    elif f <= 8:
                        zr, zi = yr * c + yi * s, yi * c - yr * s
                    else:
                        zr, zi = yr * c - yi * s, -(yi * c) - yr * s
                    out = slice(32 * f + 16 * r, 32 * f + 16 * r + 16)
                    z[out, lanes] = zr.astype(jnp.bfloat16)
                    z[out, N2 + 128 * h : N2 + 128 * h + 128] = zi.astype(jnp.bfloat16)

    transform16(*PARTS[0])

    def remote(src, dst, sems, slot, where):
        return pltpu.make_async_remote_copy(
            src_ref=src,
            dst_ref=dst,
            send_sem=sems[0].at[slot],
            recv_sem=sems[1].at[slot],
            device_id=where,
            device_id_type=MESH,
        )

    def chunk(g):
        lo, hi = PARTS[g]
        return pl.ds(lo, hi - lo)

    def far_spec(g):
        src, dst = reach.at[chunk(g), pl.ds(0, CHAN)], reach.at[chunk(g), pl.ds(2 * CHAN, CHAN)]
        return remote(src, dst, (fs_sem, fr_sem), g, at(2))

    def near_spec(g):
        lo = pl.multiple_of(odd * 2 * CHAN, CHAN)
        src, dst = reach.at[chunk(g), pl.ds(lo, CHAN)], reach.at[chunk(g), pl.ds(CHAN, CHAN)]
        return remote(src, dst, (ns_sem, nr_sem), g, mate)

    def near_grad(g):
        return remote(nsend.at[chunk(g)], nrecv.at[chunk(g)], (bns_sem, bnr_sem), g, mate)

    def back(crosses):
        return (at(-2)[0], jnp.where(crosses, 1 - band, band))

    def far_grad(g):
        rows = chunk(g), pl.ds(0, HALF)
        return remote(fsend.at[rows], frecv.at[rows], (bfs_sem, bfr_sem), g, back(lax.rem(blk, 16) < 2))

    def late_grad(i):
        rows = pl.ds(12 * i, 12 - 8 * i), pl.ds(HALF, HALF)
        return remote(fsend.at[rows], frecv.at[rows], (lbs_sem, lbr_sem), i, back(blk < 2) if i else at(-2))

    def swap(r):
        rows = pl.ds(16 * r, 16)
        return remote(csend.at[rows], crecv.at[rows], (xs_sem, xr_sem), r, partner)

    loads["dft"].wait()
    pl.semaphore_wait(barrier, 3)
    for g, (lo, hi) in enumerate(PARTS):
        if g == 1:
            transform16(lo, N1)
        s = jnp.dot(z[CHAN * lo : CHAN * hi], dft[...], preferred_element_type=jnp.float32)
        s = (s * (1.0 / math.sqrt(SAMPLES))).astype(jnp.bfloat16)
        reach[lo:hi, 0:CHAN, :] = s.reshape(hi - lo, CHAN, 2 * F2)
        far_spec(g).start()

        @pl.when(odd == 0)
        def _():
            near_spec(g).start()


    loads["pairs"].wait()
    chan_ids = lax.broadcasted_iota(jnp.int32, (128, PAIRS), 0)
    hits1 = (chan_ids == pairs_ref[0:1, :]).astype(jnp.float32)
    hits2 = (chan_ids == pairs_ref[1:2, :]).astype(jnp.float32)
    scatter = jnp.concatenate([hits1, hits2], axis=1).astype(jnp.bfloat16)[: 3 * CHAN]
    gather = jnp.concatenate([hits1.T, hits2.T], axis=0).astype(jnp.bfloat16)[:, : 3 * CHAN]

    lane_bins = lax.broadcasted_iota(jnp.int32, (1, F2), 1) * N1

    def insides(f1):
        bins = lane_bins + f1
        return [(bins >= edges_ref[n]) & (bins < edges_ref[n + 1]) for n in range(BANDS)]

    loads["edges"].wait()
    loads["tab"].wait()
    for g, (lo, hi) in enumerate(PARTS):
        far_spec(g).wait_recv()

        @pl.when(odd == 1)
        def _(g=g):
            near_spec(g).start()

        near_spec(g).wait_recv()
        for f1 in range(lo, hi):
            both = jnp.dot(gather, reach[f1], preferred_element_type=jnp.float32)
            ab[f1] = both
            ar, ai = both[:PAIRS, :F2], both[:PAIRS, F2:]
            br, bi = both[PAIRS:, :F2], both[PAIRS:, F2:]
            xr = ar * br + ai * bi
            xi = ai * br - ar * bi
            col = 2 * F2 * (f1 - lo)
            for n, inside in enumerate(insides(f1)):
                rows = slice(PAIRS * n, PAIRS * (n + 1))
                xm[rows, col : col + F2] = jnp.where(inside, xr, 0.0).astype(jnp.bfloat16)
                xm[rows, col + F2 : col + 2 * F2] = jnp.where(inside, xi, 0.0).astype(jnp.bfloat16)
        width = 2 * F2 * (hi - lo)
        part = tab[lo:hi].reshape(width, LAGS)
        term = jnp.dot(xm[:, :width], part, preferred_element_type=jnp.float32)
        if g == 0:
            corr[...] = term
        else:
            corr[...] += term

    loads["obs"].wait()
    loads["counts"].wait()
    loads["tabt"].wait()
    slot = lax.broadcasted_iota(jnp.int32, (PAIRS, 1), 0)
    live = (slot < counts_ref[0]).astype(jnp.float32)
    for n in range(BANDS):
        rows = slice(PAIRS * n, PAIRS * (n + 1))
        residual = (corr[rows] - obs[n]) * live
        wgt[rows] = (residual * (1.0 / math.sqrt(FREQ_BINS / 8.0))).astype(jnp.bfloat16)
        raw0[rows] = jnp.dot(wgt[rows], tabt[:, : 2 * F2 * PARTS[0][1]], preferred_element_type=jnp.float32)


    def lag_adjoint(g):
        lo, hi = PARTS[g]
        cols = slice(2 * F2 * lo, 2 * F2 * hi)
        out = (raw0, raw1)[g % 2]
        out[:, : 2 * F2 * (hi - lo)] = jnp.dot(wgt[...], tabt[:, cols], preferred_element_type=jnp.float32)

    def pass_on(g):
        near_grad(g).wait_recv()
        fsend[chunk(g)] = (far[chunk(g)] + nrecv[chunk(g)].astype(jnp.float32)).astype(jnp.bfloat16)
        far_grad(g).start()

    for g, (lo, hi) in enumerate(PARTS):
        if 0 < g < CHUNKS - 1:
            lag_adjoint(g + 1)
        raw = (raw0, raw1)[g % 2]
        for f1 in range(lo, hi):
            ins = [jnp.concatenate([m, m], axis=1) for m in insides(f1)]
            cols = slice(2 * F2 * (f1 - lo), 2 * F2 * (f1 - lo + 1))
            grad = jnp.where(ins[0], raw[0:PAIRS, cols], 0.0)
            grad = jnp.where(ins[1], raw[PAIRS : 2 * PAIRS, cols], grad)
            grad = jnp.where(ins[2], raw[2 * PAIRS :, cols], grad)
            gr, gi = grad[:, :F2], grad[:, F2:]
            ar, ai = ab[f1, :PAIRS, :F2], ab[f1, :PAIRS, F2:]
            br, bi = ab[f1, PAIRS:, :F2], ab[f1, PAIRS:, F2:]
            first = jnp.concatenate([gr * br - gi * bi, gr * bi + gi * br], axis=1)
            second = jnp.concatenate([gr * ar + gi * ai, gr * ai - gi * ar], axis=1)
            grads = jnp.concatenate([first, second], axis=0).astype(jnp.bfloat16)
            sums = jnp.dot(scatter, grads, preferred_element_type=jnp.float32)
            own[f1] = sums[:CHAN]
            nsend[f1] = sums[CHAN : 2 * CHAN].astype(jnp.bfloat16)
            far[f1] = sums[2 * CHAN :]
        near_grad(g).start()

        @pl.when(odd == 0)
        def _(g=g):
            fsend[chunk(g)] = far[chunk(g)].astype(jnp.bfloat16)
            far_grad(g).start()

        if g == 0:
            lag_adjoint(1)
        else:

            @pl.when(odd == 1)
            def _(g=g):
                pass_on(g - 1)

    @pl.when(odd == 1)
    def _():
        pass_on(CHUNKS - 1)

    for i in range(2):
        late_grad(i).start()

    squares = jnp.zeros((PAIRS, 1), jnp.float32)
    for n in range(BANDS):
        residual = (corr[PAIRS * n : PAIRS * (n + 1)] - obs[n]) * live
        squares = squares + jnp.sum(residual * residual, axis=1, keepdims=True)
    misfit = squares * (0.5 / (BANDS * LAGS))
    mis_ref[...] = jnp.broadcast_to(misfit, (PAIRS, PAIRS)).T[0:1]

    loads["idft"].wait()

    @pl.when(odd == 0)
    def _():
        for g in range(CHUNKS):
            near_grad(g).wait_recv()
            own[chunk(g)] += nrecv[chunk(g)].astype(jnp.float32)

    def invert(r, lo, hi):
        rows = slice(HALF * r, HALF * (r + 1))
        total = own[lo:hi, rows] + frecv[lo:hi, rows].astype(jnp.float32)
        coeffs = total.astype(jnp.bfloat16).reshape((hi - lo) * HALF, 2 * F2)
        u = jnp.dot(coeffs, idft[...], preferred_element_type=jnp.float32)
        for f1 in range(lo, hi):
            part = slice(HALF * (f1 - lo), HALF * (f1 - lo + 1))
            ur, ui = u[part, :N2], u[part, N2:]
            c, s = tw[f1, 0:1], tw[f1, 1:2]
            v[f1, 0, rows] = ur * c - ui * s
            v[f1, 1, rows] = ur * s + ui * c

    sign = (1 - 2 * band).astype(jnp.float32)
    half = N1 // 2 * N2
    my_means = []
    for r in range(CHAN // 16):
        rows = slice(16 * r, 16 * r + 16)
        if r == 0:
            for g in range(CHUNKS):
                far_grad(g).wait_recv()
                invert(0, *PARTS[g])
        else:
            for i in range(2):
                late_grad(i).wait_recv()
                invert(1, 12 * i, 12 + 4 * i)
        total_e = jnp.zeros((16, 128), jnp.float32)
        total_w = jnp.zeros((16, 128), jnp.float32)
        for h in range(N2 // 128):
            lanes = slice(128 * h, 128 * h + 128)
            vr = [v[f, 0, rows, lanes] for f in range(N1)]
            vi = [v[f, 1, rows, lanes] for f in range(N1)]
            even, odds = inverse16(vr, vi)
            for t in range(8):
                lo = N2 * t + 128 * h
                out = slice(lo, lo + 128)
                total_e = total_e + even[t]
                low, high = nf[rows, out], nf[rows, half + lo : half + lo + 128]
                total_w = total_w + (even[t] * (low + high) + odds[t] * (low - high))
                mine = odds[t] * sign
                field[rows, out] = even[t] + mine
                csend[rows, out] = (even[t] - mine).astype(jnp.bfloat16)
        mean_u = jnp.sum(total_e, axis=1, keepdims=True) * (2.0 / SAMPLES)
        mean_w = jnp.sum(total_w, axis=1, keepdims=True) * (1.0 / SAMPLES)
        my_means.append((mean_u, mean_w))
        lane = lax.broadcasted_iota(jnp.int32, (16, 128), 1)
        high_u, high_w = mean_u.astype(jnp.bfloat16).astype(jnp.float32), mean_w.astype(jnp.bfloat16).astype(jnp.float32)
        packed = jnp.where(lane == 0, high_u, jnp.where(lane == 1, mean_u - high_u, high_w))
        packed = jnp.where(lane == 3, mean_w - high_w, packed)
        csend[rows, half:] = packed.astype(jnp.bfloat16)
        swap(r).start()

    for r in range(CHAN // 16):
        rows = slice(16 * r, 16 * r + 16)
        mine = nf[rows, pl.ds(pl.multiple_of(band * half, half), half)]
        swap(r).wait_recv()
        means = crecv[rows, half:].astype(jnp.float32)
        mean_u = my_means[r][0] + (means[:, 0:1] + means[:, 1:2])
        mean_w = my_means[r][1] + (means[:, 2:3] + means[:, 3:4])
        total = field[rows] + crecv[rows, :half].astype(jnp.float32)
        adj_ref[rows] = (total - mean_u - mine * mean_w) * gain[rows]

    for g in range(CHUNKS):
        for copy in (far_spec, near_spec, near_grad, far_grad):
            copy(g).wait_send()
    for i in range(2):
        late_grad(i).wait_send()
    for r in range(CHAN // 16):
        swap(r).wait_send()


def per_device(traces, pair_list, counts, band_edges, observed):
    bf16, f32 = jnp.bfloat16, jnp.float32
    table = lag_table()
    dft = dft_table()
    tables = [
        jnp.asarray(table),
        jnp.asarray(np.ascontiguousarray(table.reshape(N1 * 2 * F2, LAGS).T)),
        jnp.asarray(dft.astype(ml_dtypes.bfloat16)),
        jnp.asarray((dft.T / math.sqrt(SAMPLES)).astype(ml_dtypes.bfloat16)),
        jnp.asarray(twiddles()),
    ]
    vmem = pl.BlockSpec(memory_space=pltpu.VMEM)
    hbm = pl.BlockSpec(memory_space=pltpu.HBM)
    dma = pltpu.SemaphoreType.DMA
    adjoint, misfit = pl.pallas_call(
        kernel,
        out_shape=(
            pltpu.VMEM((CHAN, SAMPLES // 2), f32),
            pltpu.VMEM((1, PAIRS), f32),
        ),
        in_specs=[hbm] * 10,
        out_specs=(vmem, vmem),
        scratch_shapes=[
            pltpu.VMEM((CHAN, SAMPLES), bf16),
            pltpu.VMEM((2, PAIRS), jnp.int32),
            pltpu.SMEM((1,), jnp.int32),
            pltpu.SMEM((BANDS + 1,), jnp.int32),
            pltpu.VMEM((N1, 2 * F2, LAGS), bf16),
            pltpu.VMEM((LAGS, N1 * 2 * F2), bf16),
            pltpu.VMEM((2 * N2, 2 * F2), bf16),
            pltpu.VMEM((2 * F2, 2 * N2), bf16),
            pltpu.VMEM((N1, 2, N2), f32),
            pltpu.VMEM((BANDS, PAIRS, LAGS), f32),
            pltpu.VMEM((CHAN, SAMPLES), f32),
            pltpu.VMEM((N1 * CHAN, 2 * N2), bf16),
            pltpu.VMEM((N1, 3 * CHAN, 2 * F2), bf16),
            pltpu.VMEM((N1, 2 * PAIRS, 2 * F2), f32),
            pltpu.VMEM((BANDS * PAIRS, WIDEST * 2 * F2), bf16),
            pltpu.VMEM((BANDS * PAIRS, LAGS), f32),
            pltpu.VMEM((BANDS * PAIRS, LAGS), bf16),
            pltpu.VMEM((BANDS * PAIRS, WIDEST * 2 * F2), f32),
            pltpu.VMEM((BANDS * PAIRS, WIDEST * 2 * F2), f32),
            pltpu.VMEM((N1, CHAN, 2 * F2), f32),
            pltpu.VMEM((N1, CHAN, 2 * F2), f32),
            *[pltpu.VMEM((N1, CHAN, 2 * F2), bf16)] * 4,
            *[pltpu.VMEM((CHAN, SAMPLES // 2 + 128), bf16)] * 2,
            pltpu.VMEM((N1, 2, CHAN, N2), f32),
            pltpu.VMEM((CHAN, SAMPLES // 2), f32),
            dma((10,)),
            *[dma((CHUNKS,))] * 8,
            *[dma((CHAN // 16,))] * 4,
        ],
        compiler_params=pltpu.CompilerParams(
            collective_id=0, has_side_effects=True, vmem_limit_bytes=60 << 20
        ),
        name="misfit_adjoint",
    )(traces, pair_list.T, counts, band_edges, jnp.transpose(observed, (1, 0, 2)), *tables)
    return adjoint, misfit.reshape(PAIRS)


def solution(mesh):
    in_specs = (
        P("blk", None),
        P(("blk", "band"), None),
        P(("blk", "band")),
        P(),
        P(("blk", "band"), None, None),
    )
    out_specs = (P("blk", "band"), P(("blk", "band")))
    return jax.shard_map(
        per_device, mesh=mesh, in_specs=in_specs, out_specs=out_specs, check_vma=False
    )
```

```python
import functools
import math

import jax
import jax.numpy as jnp
import ml_dtypes
import numpy as np
from jax import lax
from jax.experimental import pallas as pl
from jax.experimental.pallas import tpu as pltpu
from jax.sharding import PartitionSpec as P

SAMPLES = 4096
FREQ_BINS = 2048
MAX_LAG = 256
LAGS = 2 * MAX_LAG
BANDS = 3
CHAN = 32
PAIRS = 128
EPSILON = 1e-05
N1 = 16
N2 = 256
F2 = FREQ_BINS // N1
PARTS = ((0, 4), (4, 8), (8, 12), (12, 16))
CHUNKS = len(PARTS)
WIDEST = 4
HALF = CHAN // 2
MESH = pl.DeviceIdType.MESH


def lag_table():
    f = np.arange(N1)[:, None] + N1 * np.arange(F2)[None, :]
    shift = np.arange(-MAX_LAG, MAX_LAG)
    angle = np.mod(f[:, :, None] * shift, SAMPLES) * (2.0 * np.pi / SAMPLES)
    rows = np.stack([np.cos(angle), -np.sin(angle)], axis=1) / math.sqrt(FREQ_BINS / 8.0)
    return rows.reshape(N1, 2 * F2, LAGS).astype(ml_dtypes.bfloat16)


def dft_table():
    angle = np.mod(np.arange(N2)[:, None] * np.arange(F2)[None, :], N2) * (2.0 * np.pi / N2)
    c, s = np.cos(angle), np.sin(angle)
    return np.block([[c, -s], [s, c]])


def twiddles():
    angle = np.arange(N1)[:, None] * np.arange(N2)[None, :] * (2.0 * np.pi / SAMPLES)
    return np.stack([np.cos(angle), np.sin(angle)], axis=1).astype(np.float32)


def combine(terms):
    total = None
    for gain, value in terms:
        if abs(gain) < 1e-9:
            continue
        if abs(abs(gain) - 1.0) < 1e-9:
            if total is None:
                total = value if gain > 0 else -value
            else:
                total = total + value if gain > 0 else total - value
        else:
            scaled = value * np.float32(gain)
            total = scaled if total is None else total + scaled
    return total


def cosine(k):
    return math.cos(2.0 * math.pi * k / 16)


def sine(k):
    return math.sin(2.0 * math.pi * k / 16)


def forward16(a):
    s = [a[j] + a[j + 8] for j in range(8)]
    d = [a[j] - a[j + 8] for j in range(8)]
    out = [None] * 9
    p = [None] + [d[j] - d[8 - j] for j in range(1, 4)]
    q = [None] + [d[j] + d[8 - j] for j in range(1, 4)]
    for f in (1, 3, 5, 7):
        real = combine([(1.0, d[0])] + [(cosine(j * f), p[j]) for j in range(1, 4)])
        imag = combine([(-sine(4 * f), d[4])] + [(-sine(j * f), q[j]) for j in range(1, 4)])
        out[f] = (real, imag)
    s2 = [s[j] + s[j + 4] for j in range(4)]
    d2 = [s[j] - s[j + 4] for j in range(4)]
    for f in (2, 6):
        real = combine([(1.0, d2[0]), (cosine(f), d2[1] - d2[3])])
        imag = combine([(-sine(2 * f), d2[2]), (-sine(f), d2[1] + d2[3])])
        out[f] = (real, imag)
    out[4] = (s2[0] - s2[2], s2[3] - s2[1])
    even, odd = s2[0] + s2[2], s2[1] + s2[3]
    out[0] = (even + odd, None)
    out[8] = (even - odd, None)
    return out


def inverse16(vr, vi):
    qr = [vr[0]] + [vr[f] + vr[16 - f] for f in range(1, 8)] + [vr[8]]
    qi = [None] + [vi[f] - vi[16 - f] for f in range(1, 8)]
    even, odd = [None] * 8, [None] * 8
    for t in range(5):
        ce = combine([(cosine(t * f), qr[f]) for f in (0, 2, 4, 6, 8)])
        se = combine([(sine(t * f), qi[f]) for f in (2, 4, 6)])
        co = combine([(cosine(t * f), qr[f]) for f in (1, 3, 5, 7)])
        so = combine([(sine(t * f), qi[f]) for f in (1, 3, 5, 7)])
        even[t] = ce if se is None else ce - se
        if co is None:
            odd[t] = -so
        else:
            odd[t] = co if so is None else co - so
        if 1 <= t <= 3:
            even[8 - t] = ce + se
            odd[8 - t] = -co - so
    return even, odd


def kernel(
    x_hbm, pairs_hbm, counts_hbm, edges_hbm, obs_hbm, tab_hbm, tabt_hbm, dft_hbm, idft_hbm, tw_hbm,
    adj_ref, mis_ref,
    x_ref, pairs_ref, counts_ref, edges_ref, tab, tabt, dft, idft, tw, obs, nf, z, reach, ab, xm, corr, wgt, raw0, raw1, own, far, nsend, nrecv, fsend, frecv,
    csend, crecv, v, field,
    load_sem, fs_sem, fr_sem, ns_sem, nr_sem, bns_sem, bnr_sem, bfs_sem, bfr_sem, xs_sem, xr_sem, lbs_sem, lbr_sem,
):
    blk = lax.axis_index("blk")
    band = lax.axis_index("band")
    n_blk = lax.axis_size("blk")

    def at(step):
        return (lax.rem(blk + step + n_blk, n_blk), band)

    odd = lax.rem(blk, 2)
    mate = (blk + 1 - 2 * odd, band)
    partner = (blk, 1 - band)
    barrier = pltpu.get_barrier_semaphore()
    for where in (at(-2), mate, partner):
        pl.semaphore_signal(barrier, inc=1, device_id=where, device_id_type=MESH)

    loads = {
        name: pltpu.make_async_copy(src, dst, load_sem.at[i])
        for i, (name, src, dst) in enumerate(
            [
                ("x", x_hbm, x_ref),
                ("tw", tw_hbm, tw),
                ("pairs", pairs_hbm, pairs_ref),
                ("dft", dft_hbm, dft),
                ("edges", edges_hbm, edges_ref),
                ("counts", counts_hbm, counts_ref),
                ("tab", tab_hbm, tab),
                ("obs", obs_hbm, obs),
                ("tabt", tabt_hbm, tabt),
                ("idft", idft_hbm, idft),
            ]
        )
    }
    for load in loads.values():
        load.start()

    loads["x"].wait()
    values = x_ref[...].astype(jnp.float32)
    centred = values - jnp.mean(values, axis=1, keepdims=True)
    spread = jnp.sqrt(jnp.mean(centred * centred, axis=1, keepdims=True) + EPSILON)
    gain = 1.0 / spread
    nf[...] = centred * gain

    loads["tw"].wait()
    def transform16(lo, hi):
        for r in range(CHAN // 16):
            rows = slice(16 * r, 16 * r + 16)
            for h in range(N2 // 128):
                lanes = slice(128 * h, 128 * h + 128)
                a = [
                    nf[rows, N2 * t + 128 * h : N2 * t + 128 * h + 128].astype(jnp.bfloat16).astype(jnp.float32)
                    for t in range(N1)
                ]
                y = forward16(a)
                for f in range(lo, hi):
                    yr, yi = y[f] if f <= 8 else y[16 - f]
                    c = tw[f, 0:1, lanes]
                    s = tw[f, 1:2, lanes]
                    if yi is None:
                        zr, zi = yr * c, -(yr * s)
                    elif f <= 8:
                        zr, zi = yr * c + yi * s, yi * c - yr * s
                    else:
                        zr, zi = yr * c - yi * s, -(yi * c) - yr * s
                    out = slice(32 * f + 16 * r, 32 * f + 16 * r + 16)
                    z[out, lanes] = zr.astype(jnp.bfloat16)
                    z[out, N2 + 128 * h : N2 + 128 * h + 128] = zi.astype(jnp.bfloat16)

    transform16(*PARTS[0])

    def remote(src, dst, sems, slot, where):
        return pltpu.make_async_remote_copy(
            src_ref=src,
            dst_ref=dst,
            send_sem=sems[0].at[slot],
            recv_sem=sems[1].at[slot],
            device_id=where,
            device_id_type=MESH,
        )

    def chunk(g):
        lo, hi = PARTS[g]
        return pl.ds(lo, hi - lo)

    def far_spec(g):
        src, dst = reach.at[chunk(g), pl.ds(0, CHAN)], reach.at[chunk(g), pl.ds(2 * CHAN, CHAN)]
        return remote(src, dst, (fs_sem, fr_sem), g, at(2))

    def near_spec(g):
        lo = pl.multiple_of(odd * 2 * CHAN, CHAN)
        src, dst = reach.at[chunk(g), pl.ds(lo, CHAN)], reach.at[chunk(g), pl.ds(CHAN, CHAN)]
        return remote(src, dst, (ns_sem, nr_sem), g, mate)

    def near_grad(g):
        return remote(nsend.at[chunk(g)], nrecv.at[chunk(g)], (bns_sem, bnr_sem), g, mate)

    def back(crosses):
        return (at(-2)[0], jnp.where(crosses, 1 - band, band))

    def far_grad(g):
        rows = chunk(g), pl.ds(0, HALF)
        return remote(fsend.at[rows], frecv.at[rows], (bfs_sem, bfr_sem), g, back(lax.rem(blk, 16) < 2))

    def late_grad(i):
        rows = pl.ds(14 * i, 14 - 12 * i), pl.ds(HALF, HALF)
        return remote(fsend.at[rows], frecv.at[rows], (lbs_sem, lbr_sem), i, back(blk < 2) if i else at(-2))

    def swap(r):
        rows = pl.ds(16 * r, 16)
        return remote(csend.at[rows], crecv.at[rows], (xs_sem, xr_sem), r, partner)

    loads["dft"].wait()
    pl.semaphore_wait(barrier, 3)
    for g, (lo, hi) in enumerate(PARTS):
        if g == 1:
            transform16(lo, N1)
        s = jnp.dot(z[CHAN * lo : CHAN * hi], dft[...], preferred_element_type=jnp.float32)
        s = (s * (1.0 / math.sqrt(SAMPLES))).astype(jnp.bfloat16)
        reach[lo:hi, 0:CHAN, :] = s.reshape(hi - lo, CHAN, 2 * F2)
        far_spec(g).start()

        @pl.when(odd == 0)
        def _():
            near_spec(g).start()


    loads["pairs"].wait()
    chan_ids = lax.broadcasted_iota(jnp.int32, (128, PAIRS), 0)
    hits1 = (chan_ids == pairs_ref[0:1, :]).astype(jnp.float32)
    hits2 = (chan_ids == pairs_ref[1:2, :]).astype(jnp.float32)
    scatter = jnp.concatenate([hits1, hits2], axis=1).astype(jnp.bfloat16)[: 3 * CHAN]
    gather = jnp.concatenate([hits1.T, hits2.T], axis=0).astype(jnp.bfloat16)[:, : 3 * CHAN]

    lane_bins = lax.broadcasted_iota(jnp.int32, (1, F2), 1) * N1

    def insides(f1):
        bins = lane_bins + f1
        return [(bins >= edges_ref[n]) & (bins < edges_ref[n + 1]) for n in range(BANDS)]

    loads["edges"].wait()
    loads["tab"].wait()
    for g, (lo, hi) in enumerate(PARTS):
        far_spec(g).wait_recv()

        @pl.when(odd == 1)
        def _(g=g):
            near_spec(g).start()

        near_spec(g).wait_recv()
        for f1 in range(lo, hi):
            both = jnp.dot(gather, reach[f1], preferred_element_type=jnp.float32)
            ab[f1] = both
            ar, ai = both[:PAIRS, :F2], both[:PAIRS, F2:]
            br, bi = both[PAIRS:, :F2], both[PAIRS:, F2:]
            xr = ar * br + ai * bi
            xi = ai * br - ar * bi
            col = 2 * F2 * (f1 - lo)
            for n, inside in enumerate(insides(f1)):
                rows = slice(PAIRS * n, PAIRS * (n + 1))
                xm[rows, col : col + F2] = jnp.where(inside, xr, 0.0).astype(jnp.bfloat16)
                xm[rows, col + F2 : col + 2 * F2] = jnp.where(inside, xi, 0.0).astype(jnp.bfloat16)
        width = 2 * F2 * (hi - lo)
        part = tab[lo:hi].reshape(width, LAGS)
        term = jnp.dot(xm[:, :width], part, preferred_element_type=jnp.float32)
        if g == 0:
            corr[...] = term
        else:
            corr[...] += term

    loads["obs"].wait()
    loads["counts"].wait()
    loads["tabt"].wait()
    slot = lax.broadcasted_iota(jnp.int32, (PAIRS, 1), 0)
    live = (slot < counts_ref[0]).astype(jnp.float32)
    for n in range(BANDS):
        rows = slice(PAIRS * n, PAIRS * (n + 1))
        residual = (corr[rows] - obs[n]) * live
        wgt[rows] = (residual * (1.0 / math.sqrt(FREQ_BINS / 8.0))).astype(jnp.bfloat16)
        raw0[rows] = jnp.dot(wgt[rows], tabt[:, : 2 * F2 * PARTS[0][1]], preferred_element_type=jnp.float32)


    def lag_adjoint(g):
        lo, hi = PARTS[g]
        cols = slice(2 * F2 * lo, 2 * F2 * hi)
        out = (raw0, raw1)[g % 2]
        out[:, : 2 * F2 * (hi - lo)] = jnp.dot(wgt[...], tabt[:, cols], preferred_element_type=jnp.float32)

    def pass_on(g):
        near_grad(g).wait_recv()
        fsend[chunk(g)] = (far[chunk(g)] + nrecv[chunk(g)].astype(jnp.float32)).astype(jnp.bfloat16)
        far_grad(g).start()

    for g, (lo, hi) in enumerate(PARTS):
        if 0 < g < CHUNKS - 1:
            lag_adjoint(g + 1)
        raw = (raw0, raw1)[g % 2]
        for f1 in range(lo, hi):
            ins = [jnp.concatenate([m, m], axis=1) for m in insides(f1)]
            cols = slice(2 * F2 * (f1 - lo), 2 * F2 * (f1 - lo + 1))
            grad = jnp.where(ins[0], raw[0:PAIRS, cols], 0.0)
            grad = jnp.where(ins[1], raw[PAIRS : 2 * PAIRS, cols], grad)
            grad = jnp.where(ins[2], raw[2 * PAIRS :, cols], grad)
            gr, gi = grad[:, :F2], grad[:, F2:]
            ar, ai = ab[f1, :PAIRS, :F2], ab[f1, :PAIRS, F2:]
            br, bi = ab[f1, PAIRS:, :F2], ab[f1, PAIRS:, F2:]
            first = jnp.concatenate([gr * br - gi * bi, gr * bi + gi * br], axis=1)
            second = jnp.concatenate([gr * ar + gi * ai, gr * ai - gi * ar], axis=1)
            grads = jnp.concatenate([first, second], axis=0).astype(jnp.bfloat16)
            sums = jnp.dot(scatter, grads, preferred_element_type=jnp.float32)
            own[f1] = sums[:CHAN]
            nsend[f1] = sums[CHAN : 2 * CHAN].astype(jnp.bfloat16)
            far[f1] = sums[2 * CHAN :]
        near_grad(g).start()

        @pl.when(odd == 0)
        def _(g=g):
            fsend[chunk(g)] = far[chunk(g)].astype(jnp.bfloat16)
            far_grad(g).start()

        if g == 0:
            lag_adjoint(1)
        else:

            @pl.when(odd == 1)
            def _(g=g):
                pass_on(g - 1)

    @pl.when(odd == 1)
    def _():
        pass_on(CHUNKS - 1)

    for i in range(2):
        late_grad(i).start()

    squares = jnp.zeros((PAIRS, 1), jnp.float32)
    for n in range(BANDS):
        residual = (corr[PAIRS * n : PAIRS * (n + 1)] - obs[n]) * live
        squares = squares + jnp.sum(residual * residual, axis=1, keepdims=True)
    misfit = squares * (0.5 / (BANDS * LAGS))
    mis_ref[...] = jnp.broadcast_to(misfit, (PAIRS, PAIRS)).T[0:1]

    loads["idft"].wait()

    @pl.when(odd == 0)
    def _():
        for g in range(CHUNKS):
            near_grad(g).wait_recv()
            own[chunk(g)] += nrecv[chunk(g)].astype(jnp.float32)

    def invert(r, lo, hi):
        rows = slice(HALF * r, HALF * (r + 1))
        total = own[lo:hi, rows] + frecv[lo:hi, rows].astype(jnp.float32)
        coeffs = total.astype(jnp.bfloat16).reshape((hi - lo) * HALF, 2 * F2)
        u = jnp.dot(coeffs, idft[...], preferred_element_type=jnp.float32)
        for f1 in range(lo, hi):
            part = slice(HALF * (f1 - lo), HALF * (f1 - lo + 1))
            ur, ui = u[part, :N2], u[part, N2:]
            c, s = tw[f1, 0:1], tw[f1, 1:2]
            v[f1, 0, rows] = ur * c - ui * s
            v[f1, 1, rows] = ur * s + ui * c

    sign = (1 - 2 * band).astype(jnp.float32)
    half = N1 // 2 * N2
    my_means = []
    for r in range(CHAN // 16):
        rows = slice(16 * r, 16 * r + 16)
        if r == 0:
            for g in range(CHUNKS):
                far_grad(g).wait_recv()
                invert(0, *PARTS[g])
        else:
            for i in range(2):
                late_grad(i).wait_recv()
                invert(1, 14 * i, 14 + 2 * i)
        total_e = jnp.zeros((16, 128), jnp.float32)
        total_w = jnp.zeros((16, 128), jnp.float32)
        for h in range(N2 // 128):
            lanes = slice(128 * h, 128 * h + 128)
            vr = [v[f, 0, rows, lanes] for f in range(N1)]
            vi = [v[f, 1, rows, lanes] for f in range(N1)]
            even, odds = inverse16(vr, vi)
            for t in range(8):
                lo = N2 * t + 128 * h
                out = slice(lo, lo + 128)
                total_e = total_e + even[t]
                low, high = nf[rows, out], nf[rows, half + lo : half + lo + 128]
                total_w = total_w + (even[t] * (low + high) + odds[t] * (low - high))
                mine = odds[t] * sign
                field[rows, out] = even[t] + mine
                csend[rows, out] = (even[t] - mine).astype(jnp.bfloat16)
        mean_u = jnp.sum(total_e, axis=1, keepdims=True) * (2.0 / SAMPLES)
        mean_w = jnp.sum(total_w, axis=1, keepdims=True) * (1.0 / SAMPLES)
        my_means.append((mean_u, mean_w))
        lane = lax.broadcasted_iota(jnp.int32, (16, 128), 1)
        high_u, high_w = mean_u.astype(jnp.bfloat16).astype(jnp.float32), mean_w.astype(jnp.bfloat16).astype(jnp.float32)
        packed = jnp.where(lane == 0, high_u, jnp.where(lane == 1, mean_u - high_u, high_w))
        packed = jnp.where(lane == 3, mean_w - high_w, packed)
        csend[rows, half:] = packed.astype(jnp.bfloat16)
        swap(r).start()

    for r in range(CHAN // 16):
        rows = slice(16 * r, 16 * r + 16)
        mine = nf[rows, pl.ds(pl.multiple_of(band * half, half), half)]
        swap(r).wait_recv()
        means = crecv[rows, half:].astype(jnp.float32)
        mean_u = my_means[r][0] + (means[:, 0:1] + means[:, 1:2])
        mean_w = my_means[r][1] + (means[:, 2:3] + means[:, 3:4])
        total = field[rows] + crecv[rows, :half].astype(jnp.float32)
        adj_ref[rows] = (total - mean_u - mine * mean_w) * gain[rows]

    for g in range(CHUNKS):
        for copy in (far_spec, near_spec, near_grad, far_grad):
            copy(g).wait_send()
    for i in range(2):
        late_grad(i).wait_send()
    for r in range(CHAN // 16):
        swap(r).wait_send()


def per_device(traces, pair_list, counts, band_edges, observed):
    bf16, f32 = jnp.bfloat16, jnp.float32
    table = lag_table()
    dft = dft_table()
    tables = [
        jnp.asarray(table),
        jnp.asarray(np.ascontiguousarray(table.reshape(N1 * 2 * F2, LAGS).T)),
        jnp.asarray(dft.astype(ml_dtypes.bfloat16)),
        jnp.asarray((dft.T / math.sqrt(SAMPLES)).astype(ml_dtypes.bfloat16)),
        jnp.asarray(twiddles()),
    ]
    vmem = pl.BlockSpec(memory_space=pltpu.VMEM)
    hbm = pl.BlockSpec(memory_space=pltpu.HBM)
    dma = pltpu.SemaphoreType.DMA
    adjoint, misfit = pl.pallas_call(
        kernel,
        out_shape=(
            pltpu.VMEM((CHAN, SAMPLES // 2), f32),
            pltpu.VMEM((1, PAIRS), f32),
        ),
        in_specs=[hbm] * 10,
        out_specs=(vmem, vmem),
        scratch_shapes=[
            pltpu.VMEM((CHAN, SAMPLES), bf16),
            pltpu.VMEM((2, PAIRS), jnp.int32),
            pltpu.SMEM((1,), jnp.int32),
            pltpu.SMEM((BANDS + 1,), jnp.int32),
            pltpu.VMEM((N1, 2 * F2, LAGS), bf16),
            pltpu.VMEM((LAGS, N1 * 2 * F2), bf16),
            pltpu.VMEM((2 * N2, 2 * F2), bf16),
            pltpu.VMEM((2 * F2, 2 * N2), bf16),
            pltpu.VMEM((N1, 2, N2), f32),
            pltpu.VMEM((BANDS, PAIRS, LAGS), f32),
            pltpu.VMEM((CHAN, SAMPLES), f32),
            pltpu.VMEM((N1 * CHAN, 2 * N2), bf16),
            pltpu.VMEM((N1, 3 * CHAN, 2 * F2), bf16),
            pltpu.VMEM((N1, 2 * PAIRS, 2 * F2), f32),
            pltpu.VMEM((BANDS * PAIRS, WIDEST * 2 * F2), bf16),
            pltpu.VMEM((BANDS * PAIRS, LAGS), f32),
            pltpu.VMEM((BANDS * PAIRS, LAGS), bf16),
            pltpu.VMEM((BANDS * PAIRS, WIDEST * 2 * F2), f32),
            pltpu.VMEM((BANDS * PAIRS, WIDEST * 2 * F2), f32),
            pltpu.VMEM((N1, CHAN, 2 * F2), f32),
            pltpu.VMEM((N1, CHAN, 2 * F2), f32),
            *[pltpu.VMEM((N1, CHAN, 2 * F2), bf16)] * 4,
            *[pltpu.VMEM((CHAN, SAMPLES // 2 + 128), bf16)] * 2,
            pltpu.VMEM((N1, 2, CHAN, N2), f32),
            pltpu.VMEM((CHAN, SAMPLES // 2), f32),
            dma((10,)),
            *[dma((CHUNKS,))] * 8,
            *[dma((CHAN // 16,))] * 4,
        ],
        compiler_params=pltpu.CompilerParams(
            collective_id=0, has_side_effects=True, vmem_limit_bytes=60 << 20
        ),
        name="misfit_adjoint",
    )(traces, pair_list.T, counts, band_edges, jnp.transpose(observed, (1, 0, 2)), *tables)
    return adjoint, misfit.reshape(PAIRS)


def solution(mesh):
    in_specs = (
        P("blk", None),
        P(("blk", "band"), None),
        P(("blk", "band")),
        P(),
        P(("blk", "band"), None, None),
    )
    out_specs = (P("blk", "band"), P(("blk", "band")))
    return jax.shard_map(
        per_device, mesh=mesh, in_specs=in_specs, out_specs=out_specs, check_vma=False
    )
```

```python
import functools
import math

import jax
import jax.numpy as jnp
import ml_dtypes
import numpy as np
from jax import lax
from jax.experimental import pallas as pl
from jax.experimental.pallas import tpu as pltpu
from jax.sharding import PartitionSpec as P

SAMPLES = 4096
FREQ_BINS = 2048
MAX_LAG = 256
LAGS = 2 * MAX_LAG
BANDS = 3
CHAN = 32
PAIRS = 128
EPSILON = 1e-05
N1 = 16
N2 = 256
F2 = FREQ_BINS // N1
PARTS = ((0, 4), (4, 8), (8, 12), (12, 16))
CHUNKS = len(PARTS)
WIDEST = 4
HALF = CHAN // 2
MESH = pl.DeviceIdType.MESH


def lag_table():
    f = np.arange(N1)[:, None] + N1 * np.arange(F2)[None, :]
    shift = np.arange(-MAX_LAG, MAX_LAG)
    angle = np.mod(f[:, :, None] * shift, SAMPLES) * (2.0 * np.pi / SAMPLES)
    rows = np.stack([np.cos(angle), -np.sin(angle)], axis=1) / math.sqrt(FREQ_BINS / 8.0)
    return rows.reshape(N1, 2 * F2, LAGS).astype(ml_dtypes.bfloat16)


def dft_table():
    angle = np.mod(np.arange(N2)[:, None] * np.arange(F2)[None, :], N2) * (2.0 * np.pi / N2)
    c, s = np.cos(angle), np.sin(angle)
    return np.block([[c, -s], [s, c]])


def twiddles():
    angle = np.arange(N1)[:, None] * np.arange(N2)[None, :] * (2.0 * np.pi / SAMPLES)
    return np.stack([np.cos(angle), np.sin(angle)], axis=1).astype(np.float32)


def combine(terms):
    total = None
    for gain, value in terms:
        if abs(gain) < 1e-9:
            continue
        if abs(abs(gain) - 1.0) < 1e-9:
            if total is None:
                total = value if gain > 0 else -value
            else:
                total = total + value if gain > 0 else total - value
        else:
            scaled = value * np.float32(gain)
            total = scaled if total is None else total + scaled
    return total


def cosine(k):
    return math.cos(2.0 * math.pi * k / 16)


def sine(k):
    return math.sin(2.0 * math.pi * k / 16)


def forward16(a):
    s = [a[j] + a[j + 8] for j in range(8)]
    d = [a[j] - a[j + 8] for j in range(8)]
    out = [None] * 9
    p = [None] + [d[j] - d[8 - j] for j in range(1, 4)]
    q = [None] + [d[j] + d[8 - j] for j in range(1, 4)]
    for f in (1, 3, 5, 7):
        real = combine([(1.0, d[0])] + [(cosine(j * f), p[j]) for j in range(1, 4)])
        imag = combine([(-sine(4 * f), d[4])] + [(-sine(j * f), q[j]) for j in range(1, 4)])
        out[f] = (real, imag)
    s2 = [s[j] + s[j + 4] for j in range(4)]
    d2 = [s[j] - s[j + 4] for j in range(4)]
    for f in (2, 6):
        real = combine([(1.0, d2[0]), (cosine(f), d2[1] - d2[3])])
        imag = combine([(-sine(2 * f), d2[2]), (-sine(f), d2[1] + d2[3])])
        out[f] = (real, imag)
    out[4] = (s2[0] - s2[2], s2[3] - s2[1])
    even, odd = s2[0] + s2[2], s2[1] + s2[3]
    out[0] = (even + odd, None)
    out[8] = (even - odd, None)
    return out


def inverse16(vr, vi):
    qr = [vr[0]] + [vr[f] + vr[16 - f] for f in range(1, 8)] + [vr[8]]
    qi = [None] + [vi[f] - vi[16 - f] for f in range(1, 8)]
    even, odd = [None] * 8, [None] * 8
    for t in range(5):
        ce = combine([(cosine(t * f), qr[f]) for f in (0, 2, 4, 6, 8)])
        se = combine([(sine(t * f), qi[f]) for f in (2, 4, 6)])
        co = combine([(cosine(t * f), qr[f]) for f in (1, 3, 5, 7)])
        so = combine([(sine(t * f), qi[f]) for f in (1, 3, 5, 7)])
        even[t] = ce if se is None else ce - se
        if co is None:
            odd[t] = -so
        else:
            odd[t] = co if so is None else co - so
        if 1 <= t <= 3:
            even[8 - t] = ce + se
            odd[8 - t] = -co - so
    return even, odd


def kernel(
    x_hbm, pairs_hbm, counts_hbm, edges_hbm, obs_hbm, tab_hbm, tabt_hbm, dft_hbm, idft_hbm, tw_hbm,
    adj_ref, mis_ref,
    x_ref, pairs_ref, counts_ref, edges_ref, tab, tabt, dft, idft, tw, obs, nf, z, reach, ab, xm, corr, wgt, raw0, raw1, own, far, nsend, nrecv, fsend, frecv,
    csend, crecv, v, field,
    load_sem, fs_sem, fr_sem, ns_sem, nr_sem, bns_sem, bnr_sem, bfs_sem, bfr_sem, xs_sem, xr_sem, lbs_sem, lbr_sem,
):
    blk = lax.axis_index("blk")
    band = lax.axis_index("band")
    n_blk = lax.axis_size("blk")

    def at(step):
        return (lax.rem(blk + step + n_blk, n_blk), band)

    odd = lax.rem(blk, 2)
    mate = (blk + 1 - 2 * odd, band)
    partner = (blk, 1 - band)
    barrier = pltpu.get_barrier_semaphore()
    for where in (at(-2), mate, partner):
        pl.semaphore_signal(barrier, inc=1, device_id=where, device_id_type=MESH)

    loads = {
        name: pltpu.make_async_copy(src, dst, load_sem.at[i])
        for i, (name, src, dst) in enumerate(
            [
                ("x", x_hbm, x_ref),
                ("tw", tw_hbm, tw),
                ("pairs", pairs_hbm, pairs_ref),
                ("dft", dft_hbm, dft),
                ("edges", edges_hbm, edges_ref),
                ("counts", counts_hbm, counts_ref),
                ("tab", tab_hbm, tab),
                ("obs", obs_hbm, obs),
                ("tabt", tabt_hbm, tabt),
                ("idft", idft_hbm, idft),
            ]
        )
    }
    for load in loads.values():
        load.start()

    loads["x"].wait()
    values = x_ref[...].astype(jnp.float32)
    centred = values - jnp.mean(values, axis=1, keepdims=True)
    spread = jnp.sqrt(jnp.mean(centred * centred, axis=1, keepdims=True) + EPSILON)
    gain = 1.0 / spread
    nf[...] = centred * gain

    loads["tw"].wait()
    def transform16(lo, hi):
        for r in range(CHAN // 16):
            rows = slice(16 * r, 16 * r + 16)
            for h in range(N2 // 128):
                lanes = slice(128 * h, 128 * h + 128)
                a = [
                    nf[rows, N2 * t + 128 * h : N2 * t + 128 * h + 128].astype(jnp.bfloat16).astype(jnp.float32)
                    for t in range(N1)
                ]
                y = forward16(a)
                for f in range(lo, hi):
                    yr, yi = y[f] if f <= 8 else y[16 - f]
                    c = tw[f, 0:1, lanes]
                    s = tw[f, 1:2, lanes]
                    if yi is None:
                        zr, zi = yr * c, -(yr * s)
                    elif f <= 8:
                        zr, zi = yr * c + yi * s, yi * c - yr * s
                    else:
                        zr, zi = yr * c - yi * s, -(yi * c) - yr * s
                    out = slice(32 * f + 16 * r, 32 * f + 16 * r + 16)
                    z[out, lanes] = zr.astype(jnp.bfloat16)
                    z[out, N2 + 128 * h : N2 + 128 * h + 128] = zi.astype(jnp.bfloat16)

    transform16(*PARTS[0])

    def remote(src, dst, sems, slot, where):
        return pltpu.make_async_remote_copy(
            src_ref=src,
            dst_ref=dst,
            send_sem=sems[0].at[slot],
            recv_sem=sems[1].at[slot],
            device_id=where,
            device_id_type=MESH,
        )

    def chunk(g):
        lo, hi = PARTS[g]
        return pl.ds(lo, hi - lo)

    def far_spec(g):
        src, dst = reach.at[chunk(g), pl.ds(0, CHAN)], reach.at[chunk(g), pl.ds(2 * CHAN, CHAN)]
        return remote(src, dst, (fs_sem, fr_sem), g, at(2))

    def near_spec(g):
        lo = pl.multiple_of(odd * 2 * CHAN, CHAN)
        src, dst = reach.at[chunk(g), pl.ds(lo, CHAN)], reach.at[chunk(g), pl.ds(CHAN, CHAN)]
        return remote(src, dst, (ns_sem, nr_sem), g, mate)

    def near_grad(g):
        return remote(nsend.at[chunk(g)], nrecv.at[chunk(g)], (bns_sem, bnr_sem), g, mate)

    def back(crosses):
        return (at(-2)[0], jnp.where(crosses, 1 - band, band))

    def far_grad(g):
        rows = chunk(g), pl.ds(0, HALF)
        return remote(fsend.at[rows], frecv.at[rows], (bfs_sem, bfr_sem), g, back(lax.rem(blk, 16) < 2))

    def late_grad(i):
        rows = pl.ds(15 * i, 15 - 14 * i), pl.ds(HALF, HALF)
        return remote(fsend.at[rows], frecv.at[rows], (lbs_sem, lbr_sem), i, back(blk < 2) if i else at(-2))

    def swap(r):
        rows = pl.ds(16 * r, 16)
        return remote(csend.at[rows], crecv.at[rows], (xs_sem, xr_sem), r, partner)

    loads["dft"].wait()
    pl.semaphore_wait(barrier, 3)
    for g, (lo, hi) in enumerate(PARTS):
        if g == 1:
            transform16(lo, N1)
        s = jnp.dot(z[CHAN * lo : CHAN * hi], dft[...], preferred_element_type=jnp.float32)
        s = (s * (1.0 / math.sqrt(SAMPLES))).astype(jnp.bfloat16)
        reach[lo:hi, 0:CHAN, :] = s.reshape(hi - lo, CHAN, 2 * F2)
        far_spec(g).start()

        @pl.when(odd == 0)
        def _():
            near_spec(g).start()


    loads["pairs"].wait()
    chan_ids = lax.broadcasted_iota(jnp.int32, (128, PAIRS), 0)
    hits1 = (chan_ids == pairs_ref[0:1, :]).astype(jnp.float32)
    hits2 = (chan_ids == pairs_ref[1:2, :]).astype(jnp.float32)
    scatter = jnp.concatenate([hits1, hits2], axis=1).astype(jnp.bfloat16)[: 3 * CHAN]
    gather = jnp.concatenate([hits1.T, hits2.T], axis=0).astype(jnp.bfloat16)[:, : 3 * CHAN]

    lane_bins = lax.broadcasted_iota(jnp.int32, (1, F2), 1) * N1

    def insides(f1):
        bins = lane_bins + f1
        return [(bins >= edges_ref[n]) & (bins < edges_ref[n + 1]) for n in range(BANDS)]

    loads["edges"].wait()
    loads["tab"].wait()
    for g, (lo, hi) in enumerate(PARTS):
        far_spec(g).wait_recv()

        @pl.when(odd == 1)
        def _(g=g):
            near_spec(g).start()

        near_spec(g).wait_recv()
        for f1 in range(lo, hi):
            both = jnp.dot(gather, reach[f1], preferred_element_type=jnp.float32)
            ab[f1] = both
            ar, ai = both[:PAIRS, :F2], both[:PAIRS, F2:]
            br, bi = both[PAIRS:, :F2], both[PAIRS:, F2:]
            xr = ar * br + ai * bi
            xi = ai * br - ar * bi
            col = 2 * F2 * (f1 - lo)
            for n, inside in enumerate(insides(f1)):
                rows = slice(PAIRS * n, PAIRS * (n + 1))
                xm[rows, col : col + F2] = jnp.where(inside, xr, 0.0).astype(jnp.bfloat16)
                xm[rows, col + F2 : col + 2 * F2] = jnp.where(inside, xi, 0.0).astype(jnp.bfloat16)
        width = 2 * F2 * (hi - lo)
        part = tab[lo:hi].reshape(width, LAGS)
        term = jnp.dot(xm[:, :width], part, preferred_element_type=jnp.float32)
        if g == 0:
            corr[...] = term
        else:
            corr[...] += term

    loads["obs"].wait()
    loads["counts"].wait()
    loads["tabt"].wait()
    slot = lax.broadcasted_iota(jnp.int32, (PAIRS, 1), 0)
    live = (slot < counts_ref[0]).astype(jnp.float32)
    for n in range(BANDS):
        rows = slice(PAIRS * n, PAIRS * (n + 1))
        residual = (corr[rows] - obs[n]) * live
        wgt[rows] = (residual * (1.0 / math.sqrt(FREQ_BINS / 8.0))).astype(jnp.bfloat16)
        raw0[rows] = jnp.dot(wgt[rows], tabt[:, : 2 * F2 * PARTS[0][1]], preferred_element_type=jnp.float32)


    def lag_adjoint(g):
        lo, hi = PARTS[g]
        cols = slice(2 * F2 * lo, 2 * F2 * hi)
        out = (raw0, raw1)[g % 2]
        out[:, : 2 * F2 * (hi - lo)] = jnp.dot(wgt[...], tabt[:, cols], preferred_element_type=jnp.float32)

    def pass_on(g):
        near_grad(g).wait_recv()
        fsend[chunk(g)] = (far[chunk(g)] + nrecv[chunk(g)].astype(jnp.float32)).astype(jnp.bfloat16)
        far_grad(g).start()

    for g, (lo, hi) in enumerate(PARTS):
        if 0 < g < CHUNKS - 1:
            lag_adjoint(g + 1)
        raw = (raw0, raw1)[g % 2]
        for f1 in range(lo, hi):
            ins = [jnp.concatenate([m, m], axis=1) for m in insides(f1)]
            cols = slice(2 * F2 * (f1 - lo), 2 * F2 * (f1 - lo + 1))
            grad = jnp.where(ins[0], raw[0:PAIRS, cols], 0.0)
            grad = jnp.where(ins[1], raw[PAIRS : 2 * PAIRS, cols], grad)
            grad = jnp.where(ins[2], raw[2 * PAIRS :, cols], grad)
            gr, gi = grad[:, :F2], grad[:, F2:]
            ar, ai = ab[f1, :PAIRS, :F2], ab[f1, :PAIRS, F2:]
            br, bi = ab[f1, PAIRS:, :F2], ab[f1, PAIRS:, F2:]
            first = jnp.concatenate([gr * br - gi * bi, gr * bi + gi * br], axis=1)
            second = jnp.concatenate([gr * ar + gi * ai, gr * ai - gi * ar], axis=1)
            grads = jnp.concatenate([first, second], axis=0).astype(jnp.bfloat16)
            sums = jnp.dot(scatter, grads, preferred_element_type=jnp.float32)
            own[f1] = sums[:CHAN]
            nsend[f1] = sums[CHAN : 2 * CHAN].astype(jnp.bfloat16)
            far[f1] = sums[2 * CHAN :]
        near_grad(g).start()

        @pl.when(odd == 0)
        def _(g=g):
            fsend[chunk(g)] = far[chunk(g)].astype(jnp.bfloat16)
            far_grad(g).start()

        if g == 0:
            lag_adjoint(1)
        else:

            @pl.when(odd == 1)
            def _(g=g):
                pass_on(g - 1)

    @pl.when(odd == 1)
    def _():
        pass_on(CHUNKS - 1)

    for i in range(2):
        late_grad(i).start()

    squares = jnp.zeros((PAIRS, 1), jnp.float32)
    for n in range(BANDS):
        residual = (corr[PAIRS * n : PAIRS * (n + 1)] - obs[n]) * live
        squares = squares + jnp.sum(residual * residual, axis=1, keepdims=True)
    misfit = squares * (0.5 / (BANDS * LAGS))
    mis_ref[...] = jnp.broadcast_to(misfit, (PAIRS, PAIRS)).T[0:1]

    loads["idft"].wait()

    @pl.when(odd == 0)
    def _():
        for g in range(CHUNKS):
            near_grad(g).wait_recv()
            own[chunk(g)] += nrecv[chunk(g)].astype(jnp.float32)

    def invert(r, lo, hi):
        rows = slice(HALF * r, HALF * (r + 1))
        total = own[lo:hi, rows] + frecv[lo:hi, rows].astype(jnp.float32)
        coeffs = total.astype(jnp.bfloat16).reshape((hi - lo) * HALF, 2 * F2)
        u = jnp.dot(coeffs, idft[...], preferred_element_type=jnp.float32)
        for f1 in range(lo, hi):
            part = slice(HALF * (f1 - lo), HALF * (f1 - lo + 1))
            ur, ui = u[part, :N2], u[part, N2:]
            c, s = tw[f1, 0:1], tw[f1, 1:2]
            v[f1, 0, rows] = ur * c - ui * s
            v[f1, 1, rows] = ur * s + ui * c

    sign = (1 - 2 * band).astype(jnp.float32)
    half = N1 // 2 * N2
    my_means = []
    for r in range(CHAN // 16):
        rows = slice(16 * r, 16 * r + 16)
        if r == 0:
            for g in range(CHUNKS):
                far_grad(g).wait_recv()
                invert(0, *PARTS[g])
        else:
            for i in range(2):
                late_grad(i).wait_recv()
                invert(1, 15 * i, 15 + i)
        total_e = jnp.zeros((16, 128), jnp.float32)
        total_w = jnp.zeros((16, 128), jnp.float32)
        for h in range(N2 // 128):
            lanes = slice(128 * h, 128 * h + 128)
            vr = [v[f, 0, rows, lanes] for f in range(N1)]
            vi = [v[f, 1, rows, lanes] for f in range(N1)]
            even, odds = inverse16(vr, vi)
            for t in range(8):
                lo = N2 * t + 128 * h
                out = slice(lo, lo + 128)
                total_e = total_e + even[t]
                low, high = nf[rows, out], nf[rows, half + lo : half + lo + 128]
                total_w = total_w + (even[t] * (low + high) + odds[t] * (low - high))
                mine = odds[t] * sign
                field[rows, out] = even[t] + mine
                csend[rows, out] = (even[t] - mine).astype(jnp.bfloat16)
        mean_u = jnp.sum(total_e, axis=1, keepdims=True) * (2.0 / SAMPLES)
        mean_w = jnp.sum(total_w, axis=1, keepdims=True) * (1.0 / SAMPLES)
        my_means.append((mean_u, mean_w))
        lane = lax.broadcasted_iota(jnp.int32, (16, 128), 1)
        high_u, high_w = mean_u.astype(jnp.bfloat16).astype(jnp.float32), mean_w.astype(jnp.bfloat16).astype(jnp.float32)
        packed = jnp.where(lane == 0, high_u, jnp.where(lane == 1, mean_u - high_u, high_w))
        packed = jnp.where(lane == 3, mean_w - high_w, packed)
        csend[rows, half:] = packed.astype(jnp.bfloat16)
        swap(r).start()

    for r in range(CHAN // 16):
        rows = slice(16 * r, 16 * r + 16)
        mine = nf[rows, pl.ds(pl.multiple_of(band * half, half), half)]
        swap(r).wait_recv()
        means = crecv[rows, half:].astype(jnp.float32)
        mean_u = my_means[r][0] + (means[:, 0:1] + means[:, 1:2])
        mean_w = my_means[r][1] + (means[:, 2:3] + means[:, 3:4])
        total = field[rows] + crecv[rows, :half].astype(jnp.float32)
        adj_ref[rows] = (total - mean_u - mine * mean_w) * gain[rows]

    for g in range(CHUNKS):
        for copy in (far_spec, near_spec, near_grad, far_grad):
            copy(g).wait_send()
    for i in range(2):
        late_grad(i).wait_send()
    for r in range(CHAN // 16):
        swap(r).wait_send()


def per_device(traces, pair_list, counts, band_edges, observed):
    bf16, f32 = jnp.bfloat16, jnp.float32
    table = lag_table()
    dft = dft_table()
    tables = [
        jnp.asarray(table),
        jnp.asarray(np.ascontiguousarray(table.reshape(N1 * 2 * F2, LAGS).T)),
        jnp.asarray(dft.astype(ml_dtypes.bfloat16)),
        jnp.asarray((dft.T / math.sqrt(SAMPLES)).astype(ml_dtypes.bfloat16)),
        jnp.asarray(twiddles()),
    ]
    vmem = pl.BlockSpec(memory_space=pltpu.VMEM)
    hbm = pl.BlockSpec(memory_space=pltpu.HBM)
    dma = pltpu.SemaphoreType.DMA
    adjoint, misfit = pl.pallas_call(
        kernel,
        out_shape=(
            pltpu.VMEM((CHAN, SAMPLES // 2), f32),
            pltpu.VMEM((1, PAIRS), f32),
        ),
        in_specs=[hbm] * 10,
        out_specs=(vmem, vmem),
        scratch_shapes=[
            pltpu.VMEM((CHAN, SAMPLES), bf16),
            pltpu.VMEM((2, PAIRS), jnp.int32),
            pltpu.SMEM((1,), jnp.int32),
            pltpu.SMEM((BANDS + 1,), jnp.int32),
            pltpu.VMEM((N1, 2 * F2, LAGS), bf16),
            pltpu.VMEM((LAGS, N1 * 2 * F2), bf16),
            pltpu.VMEM((2 * N2, 2 * F2), bf16),
            pltpu.VMEM((2 * F2, 2 * N2), bf16),
            pltpu.VMEM((N1, 2, N2), f32),
            pltpu.VMEM((BANDS, PAIRS, LAGS), f32),
            pltpu.VMEM((CHAN, SAMPLES), f32),
            pltpu.VMEM((N1 * CHAN, 2 * N2), bf16),
            pltpu.VMEM((N1, 3 * CHAN, 2 * F2), bf16),
            pltpu.VMEM((N1, 2 * PAIRS, 2 * F2), f32),
            pltpu.VMEM((BANDS * PAIRS, WIDEST * 2 * F2), bf16),
            pltpu.VMEM((BANDS * PAIRS, LAGS), f32),
            pltpu.VMEM((BANDS * PAIRS, LAGS), bf16),
            pltpu.VMEM((BANDS * PAIRS, WIDEST * 2 * F2), f32),
            pltpu.VMEM((BANDS * PAIRS, WIDEST * 2 * F2), f32),
            pltpu.VMEM((N1, CHAN, 2 * F2), f32),
            pltpu.VMEM((N1, CHAN, 2 * F2), f32),
            *[pltpu.VMEM((N1, CHAN, 2 * F2), bf16)] * 4,
            *[pltpu.VMEM((CHAN, SAMPLES // 2 + 128), bf16)] * 2,
            pltpu.VMEM((N1, 2, CHAN, N2), f32),
            pltpu.VMEM((CHAN, SAMPLES // 2), f32),
            dma((10,)),
            *[dma((CHUNKS,))] * 8,
            *[dma((CHAN // 16,))] * 4,
        ],
        compiler_params=pltpu.CompilerParams(
            collective_id=0, has_side_effects=True, vmem_limit_bytes=60 << 20
        ),
        name="misfit_adjoint",
    )(traces, pair_list.T, counts, band_edges, jnp.transpose(observed, (1, 0, 2)), *tables)
    return adjoint, misfit.reshape(PAIRS)


def solution(mesh):
    in_specs = (
        P("blk", None),
        P(("blk", "band"), None),
        P(("blk", "band")),
        P(),
        P(("blk", "band"), None, None),
    )
    out_specs = (P("blk", "band"), P(("blk", "band")))
    return jax.shard_map(
        per_device, mesh=mesh, in_specs=in_specs, out_specs=out_specs, check_vma=False
    )
```
